512 devices in a mesh: member: 32 (over z_hi, y, core), tensor: 16 (over x, z_lo).
Axes of the slice: x: 4, y: 4, z: 16 (z_hi: 4, z_lo: 4; z = z_hi * 4 + z_lo), core: 2. Of those that a mesh axis runs over, the one named last changes fastest.
Arguments:
- features: bfloat16 [6144, 16384], P('member', 'tensor'), may hold values from -6 to 6
- down_weight: bfloat16 [5120, 16384], P('member', 'tensor'), may hold values from -0.09375 to 0.09375
- member_left: bfloat16 [1024, 5120], P('member'), may hold values from -6 to 6
- member_right: bfloat16 [1024, 16384], P('member', 'tensor'), may hold values from -6 to 6
- probe: float32 [5120], P('tensor'), may hold values from -16 to 16
- payoff: float32 [1024], replicated, may hold values from 0.5 to 2
- opponent: int32 [1024], replicated, may hold values from 0 to 1023, each once
Outputs:
- mixed: bfloat16 [6144, 5120], P('member', 'tensor')
- weight_step: float32 [5120, 16384], P('member', 'tensor')
The draws below stay inside these ranges and needn't reach their ends.
Inputs may be any that keep to these rules, and one draw needn't show every extreme that they name: Each member index appears exactly once as an opponent.
All inputs are finite; a program needn't handle non-finite values.
Results may differ from the reference program's by a relative error of at most 0.017.
Values may be sent and summed in bfloat16 or wider, within the bound.
No kernel may reach another device: no remote copies, remote signals or barrier semaphores. Data moves between devices by JAX's collectives and lax.ppermute only.
A program may use at most 64 MiB of HBM per device.

```python
import math
import jax
import jax.numpy as jnp
from jax import lax

D = 5120
FF = 16384
TOK = 6
POP = 1024
N_TENSOR = 16


def draw_probe(key, part):
    key = jax.random.fold_in(key, 5)
    level = jnp.arange(D, dtype=jnp.float32) / (D - 1)
    base = jnp.clip(jax.random.normal(key, (D,), jnp.float32), -4.0, 4.0)
    return base * jnp.power(3.0, level)


def with_spikes(values, key, source, target, blocks, factor):
    owner, partner = [(jnp.arange(values.shape[dim]) // (values.shape[dim] // blocks)).reshape([-1 if axis == dim else 1 for axis in range(values.ndim)]) for dim in (source, target)]
    chosen = jax.random.permutation(key, blocks)[partner]
    strong = (owner == chosen) | (owner == (partner + blocks // 2) % blocks)
    return jnp.where(strong, factor * values, values)


def block_scale(own_key, extent, split, low, high):
    gain, own = 1.0, jax.random.fold_in(own_key, 6)
    for position, blocks in split:
        heights = jnp.exp(jax.random.uniform(jax.random.fold_in(own, position), (blocks,), jnp.float32, low / len(split), high / len(split)))
        gain = gain * jnp.repeat(heights, extent[position] // blocks).reshape([-1 if axis == position else 1 for axis in range(len(extent))])
    return gain


def gaussian(key, extent, scale, bound, pieces=(), kind=jnp.bfloat16):
    loudness = block_scale(key, extent, pieces, -0.22, 0.18) if pieces else 1.0
    array = jax.random.normal(key, extent, jnp.float32) * scale * loudness
    return jnp.minimum(jnp.maximum(array, -bound), bound).astype(kind)


def noise_with(rng, dims, scale, most, shards, heavy, held_as=jnp.bfloat16):
    array = scale * jax.random.normal(rng, dims, jnp.float32)
    if shards:
        array = array * block_scale(rng, dims, shards, -0.22, 0.18)
    return jnp.clip(with_spikes(array, jax.random.fold_in(rng, 3), *heavy), -most, most).astype(held_as)


def setup_inputs(seed: int = 0) -> dict:
    arg_keys = jax.random.split(jax.random.key(seed), 8)
    features = gaussian(arg_keys[0], (POP * TOK, FF), 1.0, 6.0, ((0, 32), (1, 16)))
    down_weight = noise_with(arg_keys[1], (D, FF), FF ** -0.5, 0.09375, ((0, 32), (1, 16)), (1, 0, 32, 2.75))
    member_left = gaussian(arg_keys[2], (POP, D), 1.0, 6.0, ((0, 32),))
    member_right = gaussian(arg_keys[3], (POP, FF), 1.0, 6.0, ((0, 32), (1, 16)))
    probe = draw_probe(jax.random.fold_in(arg_keys[7], 71), 0)
    payoff = jnp.clip(jnp.exp(jax.random.uniform(arg_keys[5], (POP,), jnp.float32, math.log(0.5), math.log(2.0))), 0.5, 2.0)
    opponent = jax.random.permutation(arg_keys[6], POP).astype(jnp.int32)
    return dict(features=features, down_weight=down_weight, member_left=member_left, member_right=member_right, probe=probe, payoff=payoff, opponent=opponent)


def reference(features, down_weight, member_left, member_right, probe, payoff, opponent):
    width = FF // N_TENSOR
    spread = 1.0 / jnp.sqrt(jnp.float32(FF))
    left_wide = member_left.astype(jnp.float32)

    def add_block(total, index):
        begin = (index * width).astype(jnp.int32)
        cols = lax.dynamic_slice_in_dim(features, begin, width, 1)
        wcols = lax.dynamic_slice_in_dim(down_weight, begin, width, 1)
        rights = lax.dynamic_slice_in_dim(member_right, begin, width, 1)
        base = lax.dot_general(cols, wcols, (((1,), (1,)), ((), ())), preferred_element_type=jnp.float32)
        inner = jnp.einsum('mtf,mf->mt', cols.reshape(POP, TOK, width).astype(jnp.float32), rights.astype(jnp.float32))
        lowrank = (spread * inner)[:, :, None] * left_wide[:, None, :]
        part = (base + lowrank.reshape(POP * TOK, D)).astype(jnp.bfloat16)
        part = lax.optimization_barrier(part)
        return (total + part.astype(jnp.float32), None)
    start = jnp.zeros((POP * TOK, D), jnp.float32)
    total, _ = lax.scan(add_block, start, jnp.arange(N_TENSOR, dtype=jnp.int32))
    mixed = total.astype(jnp.bfloat16)
    dots = lax.optimization_barrier(jnp.sum(total * probe[None, :], axis=1))
    score = lax.optimization_barrier(jnp.mean(jnp.tanh(0.5 * dots / jnp.sqrt(jnp.float32(D))).reshape(POP, TOK), axis=1))
    fitness = payoff * (score - score[opponent])
    scaled = (fitness[:, None] * left_wide).astype(jnp.bfloat16)
    step = jnp.dot(scaled.T, member_right, preferred_element_type=jnp.float32)
    weight_step = step / jnp.sqrt(jnp.float32(POP))
    return (mixed, weight_step)
```

```python
import jax
import jax.numpy as jnp
from jax import lax
from jax.sharding import Mesh, PartitionSpec as P

D = 5120
FF = 16384
AXES = ("zh", "y", "c", "x", "zl")
SIZES = (4, 4, 2, 4, 4)


def place(*index):
    at = 0
    for i, size in zip(index, SIZES):
        at = at * size + i
    return at


def ring(step):
    return [(i, (i + step) % 4) for i in range(4)]


def swapped(flip):
    return [
        (place(zh, y, c, x, zl), place(x, zl, c ^ flip, zh, y))
        for zh in range(4) for y in range(4) for c in range(2) for x in range(4) for zl in range(4)
    ]


def turned(flip):
    return [
        ((y * 2 + c) * 4 + zl, (zl * 2 + (c ^ flip)) * 4 + y)
        for y in range(4) for c in range(2) for zl in range(4)
    ]


def move(value, axis, step):
    return lax.ppermute(value, axis, ring(step))


def per_device(features, down_weight, member_left, member_right, probe, payoff, opponent):
    f32, bf16 = jnp.float32, jnp.bfloat16
    rows, width = features.shape
    members = member_right.shape[0]
    tokens = rows // members
    population = payoff.shape[0]
    block = down_weight.shape[0]
    cols = probe.shape[0]
    spread = 1.0 / jnp.sqrt(f32(FF))
    zh, y, c, x, zl = (lax.axis_index(a) for a in AXES)
    first = c == 0

    own = jnp.concatenate([down_weight, member_right], axis=0)
    cut = own.shape[0] // 2
    before = move(own, "zh", 1)
    after = move(own, "zh", -1)
    gathered = lax.all_gather(features, ("y", "c"), axis=0, tiled=True)
    far = jnp.concatenate([move(before[:cut], "zh", 1), move(after[cut:], "zh", -1)], axis=0)

    left_cols = lax.dynamic_slice(member_left, (0, (x * 4 + zl) * cols), (members, cols)).astype(f32)
    payload = jnp.concatenate([left_cols, probe[None, :]], axis=0)
    mine = jnp.where(first, payload[:, :block], payload[:, block:])
    other = jnp.where(first, payload[:, block:], payload[:, :block])
    mine = lax.ppermute(mine, AXES, swapped(0))
    other = lax.ppermute(other, AXES, swapped(1))
    left_mine = mine[:members].astype(bf16)
    left_other = other[:members].astype(bf16)
    left_pair = jnp.where(
        first, jnp.concatenate([left_mine, left_other], 0), jnp.concatenate([left_other, left_mine], 0)
    )
    left_all = lax.all_gather(left_pair, ("x", "zl"), axis=0, tiled=True)

    direction = jnp.sum(down_weight.astype(f32) * mine[members][:, None], axis=0)
    direction = lax.psum(lax.psum(direction, ("y", "c")), "zh")
    wide = features.astype(f32)
    along = jnp.sum(wide * direction[None, :], axis=1)
    inner = jnp.sum(
        wide.reshape(members, tokens, width) * member_right.astype(f32)[:, None, :], axis=2
    ).reshape(rows)
    left_dot = jnp.sum(left_cols * probe[None, :], axis=1)
    sums = jnp.concatenate([along, inner, left_dot])
    sums = lax.psum(lax.psum(sums, "x"), "zl")
    along, inner, left_dot = sums[:rows], spread * sums[rows : 2 * rows], sums[2 * rows :]
    dots = along + inner * jnp.repeat(left_dot, tokens)
    scale = 0.5 / jnp.sqrt(f32(D))
    own_score = jnp.mean(jnp.tanh(scale * dots).reshape(members, tokens), axis=1)
    score = lax.dynamic_update_slice(
        jnp.zeros((population,), f32), own_score, (((zh * 4 + y) * 2 + c) * members,)
    )
    score = lax.psum(lax.psum(score, ("y", "c")), "zh")
    labels = jnp.arange(population, dtype=jnp.int32)
    rival = jnp.sum(jnp.where(opponent[:, None] == labels[None, :], score[None, :], 0.0), axis=1)
    fitness = payoff * (score - rival)

    stack = jnp.stack([own, after, far, before])
    parts = []
    for k in range(4):
        weight = lax.dynamic_index_in_dim(stack, lax.rem(x + k + 4 - zh, 4), 0, keepdims=False)[:block]
        part = lax.dot_general(
            weight, gathered, (((1,), (1,)), ((), ())), preferred_element_type=f32
        ).astype(bf16)
        parts.append(part if k == 0 else move(part, "x", k))
    total = sum(p.astype(f32) for p in parts).astype(bf16)
    span = 2 * rows
    parts = []
    for k in range(4):
        part = lax.dynamic_slice(total, (0, lax.rem(zl + k, 4) * span), (block, span))
        parts.append(part if k == 0 else move(part, "zl", k))
    total = sum(p.astype(f32) for p in parts).astype(bf16)
    low, high = total[:, :rows], total[:, rows:]
    same = lax.ppermute(jnp.where(first, low, high), ("y", "c", "zl"), turned(0))
    cross = lax.ppermute(jnp.where(first, high, low), ("y", "c", "zl"), turned(1))
    total = jnp.where(
        first, jnp.concatenate([same, cross], 0), jnp.concatenate([cross, same], 0)
    ).astype(f32).T
    lowrank = inner.reshape(members, tokens)[:, :, None] * left_cols[:, None, :]
    mixed = (total + lowrank.reshape(rows, cols)).astype(bf16)

    rights = jnp.roll(stack[:, block:], zh, axis=0)
    right_all = lax.all_gather(rights, ("y", "c"), axis=0, tiled=False)
    scaled = (fitness[:, None] * left_all.astype(f32)).astype(bf16)
    scaled = scaled.reshape(4, 8, members, block).transpose(1, 0, 2, 3).reshape(population, block)
    term = lax.dot_general(
        scaled, right_all.reshape(population, width), (((0,), (0,)), ((), ())),
        preferred_element_type=f32,
    )
    return mixed, term / jnp.sqrt(f32(population))


def solution(mesh):
    fine = Mesh(mesh.devices.reshape(SIZES), AXES)
    member, tensor = ("zh", "y", "c"), ("x", "zl")
    in_specs = (
        P(member, tensor), P(member, tensor), P(member, None), P(member, tensor), P(tensor), P(), P(),
    )
    out_specs = (P(member, tensor), P(member, tensor))
    return jax.shard_map(
        per_device, mesh=fine, in_specs=in_specs, out_specs=out_specs, check_vma=False
    )
```

```python
import jax
import jax.numpy as jnp
from jax import lax
from jax.sharding import Mesh, PartitionSpec as P

D = 5120
FF = 16384
AXES = ("zh", "y", "c", "x", "zl")
SIZES = (4, 4, 2, 4, 4)


def place(*index):
    at = 0
    for i, size in zip(index, SIZES):
        at = at * size + i
    return at


def ring(step):
    return [(i, (i + step) % 4) for i in range(4)]


def swapped(flip):
    return [
        (place(zh, y, c, x, zl), place(x, zl, c ^ flip, zh, y))
        for zh in range(4) for y in range(4) for c in range(2) for x in range(4) for zl in range(4)
    ]


def turned(flip):
    return [
        ((y * 2 + c) * 4 + zl, (zl * 2 + (c ^ flip)) * 4 + y)
        for y in range(4) for c in range(2) for zl in range(4)
    ]


def move(value, axis, step):
    return lax.ppermute(value, axis, ring(step))


def added(value, axis):
    return value + move(value, axis, 1) + move(value, axis, -1) + move(value, axis, 2)


def around(value, axis, index):
    stack = jnp.stack([value, move(value, axis, -1), move(value, axis, 2), move(value, axis, 1)])
    return jnp.roll(stack, index, axis=0)


def in_three(value):
    terms = []
    for _ in range(3):
        term = lax.reduce_precision(value, 8, 7)
        terms.append(term.astype(jnp.bfloat16))
        value = value - term
    return jnp.stack(terms)


def per_device(features, down_weight, member_left, member_right, probe, payoff, opponent):
    f32, bf16 = jnp.float32, jnp.bfloat16
    rows, width = features.shape
    members = member_right.shape[0]
    tokens = rows // members
    population = payoff.shape[0]
    block = down_weight.shape[0]
    cols = probe.shape[0]
    spread = 1.0 / jnp.sqrt(f32(FF))
    zh, y, c, x, zl = (lax.axis_index(a) for a in AXES)
    first = c == 0
    group = 8

    gathered = lax.all_gather(features, ("y", "c"), axis=0, tiled=True)

    lead = (block + members) // 2
    chunks = []
    for own in (down_weight[:lead], jnp.concatenate([down_weight[lead:], member_right], axis=0)):
        cut = own.shape[0] // 2
        before = move(own, "zh", 1)
        after = move(own, "zh", -1)
        far = [move(before[:cut], "zh", 1), move(after[cut:], "zh", -1)]
        chunks.append(jnp.concatenate([own, after] + far + [before], axis=0).reshape(4, lead, width))
    weights = [chunks[0], chunks[1][:, : block - lead]]
    rights = chunks[1][:, block - lead :]

    probes = around(probe, "x", x)
    probes = jnp.where(first, probes[:, :block], probes[:, block:])
    probes = lax.ppermute(probes, ("y", "c", "zl"), turned(0))
    probes = in_three(jnp.roll(probes, -zh, axis=0))
    direction = 0.0
    for weight, start in zip(weights, (0, lead)):
        part = probes[:, :, start : start + weight.shape[1]].reshape(3, -1)
        direction += lax.dot_general(
            part, weight.reshape(-1, width), (((1,), (0,)), ((), ())), preferred_element_type=f32
        ).sum(0)

    left_cols = lax.dynamic_slice(member_left, (0, (x * 4 + zl) * cols), (members, cols))
    mine = jnp.where(first, left_cols[:, :block], left_cols[:, block:])
    other = jnp.where(first, left_cols[:, block:], left_cols[:, :block])
    mine = lax.ppermute(mine, AXES, swapped(0))
    other = lax.ppermute(other, AXES, swapped(1))
    left_all = jnp.where(
        first, jnp.concatenate([mine, other], 0), jnp.concatenate([other, mine], 0)
    )
    left_all = around(around(left_all, "x", x), "zl", zl)

    left_cols = left_cols.astype(f32)
    along = lax.dot_general(
        in_three(direction), gathered, (((1,), (1,)), ((), ())), preferred_element_type=f32
    ).sum(0)
    inner = jnp.sum(
        features.astype(f32).reshape(members, tokens, width) * member_right.astype(f32)[:, None, :],
        axis=2,
    ).reshape(rows)
    left_dot = jnp.sum(left_cols * probe[None, :], axis=1)
    here = y * 2 + c
    inner = lax.dynamic_update_slice(jnp.zeros((group * rows,), f32), inner, (here * rows,))
    left_dot = lax.dynamic_update_slice(
        jnp.zeros((group * members,), f32), left_dot, (here * members,)
    )
    sums = jnp.concatenate([along, inner, left_dot])
    sums = sums + lax.ppermute(sums, "c", [(0, 1), (1, 0)])
    sums = added(added(added(sums, "y"), "x"), "zl")
    along, inner, left_dot = jnp.split(sums, [group * rows, 2 * group * rows])
    inner = spread * inner
    dots = along + inner * jnp.repeat(left_dot, tokens)
    scale = 0.5 / jnp.sqrt(f32(D))
    score = jnp.mean(jnp.tanh(scale * dots).reshape(group * members, tokens), axis=1)
    score = around(score, "zh", zh).reshape(population)
    labels = jnp.arange(population, dtype=jnp.int32)
    rival = jnp.sum(jnp.where(opponent[:, None] == labels[None, :], score[None, :], 0.0), axis=1)
    fitness = payoff * (score - rival)

    totals = []
    for weight in weights:
        parts = []
        for k in range(4):
            part = lax.dynamic_index_in_dim(weight, lax.rem(x + k + 4 - zh, 4), 0, keepdims=False)
            part = lax.dot_general(
                part, gathered, (((1,), (1,)), ((), ())), preferred_element_type=f32
            ).astype(bf16)
            parts.append(part if k == 0 else move(part, "x", k))
        totals.append(sum(p.astype(f32) for p in parts).astype(bf16))
    total = jnp.concatenate(totals, axis=0)
    span = 2 * rows
    parts = []
    for k in range(4):
        part = lax.dynamic_slice(total, (0, lax.rem(zl + k, 4) * span), (block, span))
        parts.append(part if k == 0 else move(part, "zl", k))
    total = sum(p.astype(f32) for p in parts).astype(bf16)
    low, high = total[:, :rows], total[:, rows:]
    same = lax.ppermute(jnp.where(first, low, high), ("y", "c", "zl"), turned(0))
    cross = lax.ppermute(jnp.where(first, high, low), ("y", "c", "zl"), turned(1))
    total = jnp.where(
        first, jnp.concatenate([same, cross], 0), jnp.concatenate([cross, same], 0)
    ).astype(f32).T
    own_inner = lax.dynamic_slice(inner, (here * rows,), (rows,))
    lowrank = own_inner.reshape(members, tokens)[:, :, None] * left_cols[:, None, :]
    mixed = (total + lowrank.reshape(rows, cols)).astype(bf16)

    right_all = lax.all_gather(jnp.roll(rights, zh, axis=0), ("y", "c"), axis=0, tiled=False)
    scaled = left_all.reshape(4, 4, 2, members, block).transpose(0, 2, 1, 3, 4).astype(f32)
    fitness = fitness.reshape(4, 4, 2, members).transpose(1, 2, 0, 3)
    scaled = (fitness[..., None] * scaled).astype(bf16).reshape(population, block)
    term = lax.dot_general(
        scaled, right_all.reshape(population, width), (((0,), (0,)), ((), ())),
        preferred_element_type=f32,
    )
    return mixed, term / jnp.sqrt(f32(population))


def solution(mesh):
    fine = Mesh(mesh.devices.reshape(SIZES), AXES)
    member, tensor = ("zh", "y", "c"), ("x", "zl")
    in_specs = (
        P(member, tensor), P(member, tensor), P(member, None), P(member, tensor), P(tensor), P(), P(),
    )
    out_specs = (P(member, tensor), P(member, tensor))
    return jax.shard_map(
        per_device, mesh=fine, in_specs=in_specs, out_specs=out_specs, check_vma=False
    )
```

```python
import jax
import jax.numpy as jnp
from jax import lax
from jax.sharding import Mesh, PartitionSpec as P

D = 5120
FF = 16384
AXES = ("zh", "y", "c", "x", "zl")
SIZES = (4, 4, 2, 4, 4)


def place(*index):
    at = 0
    for i, size in zip(index, SIZES):
        at = at * size + i
    return at


def ring(step):
    return [(i, (i + step) % 4) for i in range(4)]


def swapped(flip):
    return [
        (place(zh, y, c, x, zl), place(x, zl, c ^ flip, zh, y))
        for zh in range(4) for y in range(4) for c in range(2) for x in range(4) for zl in range(4)
    ]


def turned(flip):
    return [
        ((y * 2 + c) * 4 + zl, (zl * 2 + (c ^ flip)) * 4 + y)
        for y in range(4) for c in range(2) for zl in range(4)
    ]


def move(value, axis, step):
    return lax.ppermute(value, axis, ring(step))


def pairs(step):
    return [(i, i ^ step) for i in range(4)]


def added(value, axis):
    value = value + lax.ppermute(value, axis, pairs(1))
    return value + lax.ppermute(value, axis, pairs(3))


def joined(value, axis, index):
    for step, later in ((1, index % 2 == 1), (3, index >= 2)):
        got = lax.ppermute(value, axis, pairs(step))
        value = jnp.concatenate([jnp.where(later, got, value), jnp.where(later, value, got)], axis=0)
    return value


def in_three(value):
    terms = []
    for _ in range(3):
        term = lax.reduce_precision(value, 8, 7)
        terms.append(term.astype(jnp.bfloat16))
        value = value - term
    return jnp.stack(terms)


def pack(along, inner, left_dot):
    last = in_three(left_dot).reshape(1, -1)
    last = jnp.pad(last, ((0, 1), (0, along.shape[0] - last.shape[1])))
    return jnp.concatenate([in_three(along), in_three(inner), last], axis=0)


def unpack(rows, few):
    return rows[:3].sum(0), rows[3:6].sum(0), rows[6, : 3 * few].reshape(3, few).sum(0)


def per_device(features, down_weight, member_left, member_right, probe, payoff, opponent):
    f32, bf16 = jnp.float32, jnp.bfloat16
    rows, width = features.shape
    members = member_right.shape[0]
    tokens = rows // members
    population = payoff.shape[0]
    block = down_weight.shape[0]
    cols = probe.shape[0]
    spread = 1.0 / jnp.sqrt(f32(FF))
    zh, y, c, x, zl = (lax.axis_index(a) for a in AXES)
    first = c == 0
    group = 8
    few, many = group * members, group * rows
    here = y * 2 + c

    gathered = lax.all_gather(features, ("y", "c"), axis=0, tiled=True)

    def around_z(own):
        cut = own.shape[0] // 2
        before = move(own, "zh", 1)
        after = move(own, "zh", -1)
        far = [move(before[:cut], "zh", 1), move(after[cut:], "zh", -1)]
        both = jnp.concatenate([own, after] + far + [before], axis=0).reshape(4, *own.shape)
        return both, before, after

    def products(weight):
        part = lax.dot_general(
            weight.reshape(-1, width), gathered, (((1,), (1,)), ((), ())),
            preferred_element_type=f32,
        ).astype(bf16).reshape(4, -1, many)
        return [
            lax.dynamic_index_in_dim(part, lax.rem(x + k + 4 - zh, 4), 0, keepdims=False)
            for k in range(4)
        ]

    def over_x(parts, extra):
        parts = [jnp.concatenate([p, extra], axis=0) for p in parts]
        return [parts[0]] + [move(parts[k], "x", k) for k in (1, 2, 3)]

    left_cols = lax.dynamic_slice(member_left, (0, (x * 4 + zl) * cols), (members, cols)).astype(f32)
    payload = jnp.concatenate([left_cols, probe[None, :]], axis=0)
    mine = jnp.where(first, payload[:, :block], payload[:, block:])
    other = jnp.where(first, left_cols[:, block:], left_cols[:, :block])
    mine = lax.ppermute(mine, AXES, swapped(0))
    other = lax.ppermute(other, AXES, swapped(1))

    lead = 112
    weight_one, before, after = around_z(down_weight[:lead])

    direction = jnp.sum(down_weight.astype(f32) * mine[members][:, None], axis=0)
    inner = jnp.sum(
        features.astype(f32).reshape(members, tokens, width) * member_right.astype(f32)[:, None, :],
        axis=2,
    ).reshape(rows)
    left_dot = jnp.sum(left_cols * probe[None, :], axis=1)
    inner = lax.dynamic_update_slice(jnp.zeros((many,), f32), inner, (here * rows,))
    left_dot = lax.dynamic_update_slice(jnp.zeros((few,), f32), left_dot, (here * members,))
    early = jnp.concatenate([direction, inner, left_dot])
    early, _, _ = lax.optimization_barrier((early, before, after))
    early = early + lax.ppermute(early, "c", [(0, 1), (1, 0)])
    early = added(early, "y")
    direction, inner, left_dot = jnp.split(early, [width, width + many])

    direction = jnp.pad(in_three(direction), ((0, 5), (0, 0)))
    rest = block - lead
    two, _, _ = around_z(jnp.concatenate([down_weight[lead:], member_right, direction], axis=0))
    weight_two, rights, direction = jnp.split(two, [rest, rest + members], axis=1)

    mine, other = mine[:members], other
    lefts = jnp.where(first, jnp.concatenate([mine, other], 0), jnp.concatenate([other, mine], 0))
    lefts = jnp.pad(lefts.astype(bf16), ((0, 0), (0, 192 - block))).reshape(8, many)
    parts = over_x(products(weight_one), lefts)
    weight_two, parts[1] = lax.optimization_barrier((weight_two, parts[1]))
    total_one = sum(p[:lead].astype(f32) for p in parts).astype(bf16)
    lefts = jnp.stack([parts[k][lead:] for k in (0, 3, 2, 1)])

    along = lax.dot_general(
        in_three(direction.astype(f32).sum((0, 1))), gathered, (((1,), (1,)), ((), ())),
        preferred_element_type=f32,
    ).sum(0)
    parts = over_x(products(weight_two), pack(along, inner, left_dot))
    total_two = sum(p.astype(f32) for p in parts)
    lefts, total_two = lax.optimization_barrier((lefts, total_two))
    lefts = joined(jnp.roll(lefts, x, axis=0).reshape(-1, many), "zl", zl)
    sums = pack(*unpack(total_two[rest:], few)).reshape(-1, 2 * rows)
    total = jnp.concatenate([total_one, total_two[:rest].astype(bf16)], axis=0)
    span = 2 * rows
    parts = []
    for k in range(4):
        part = lax.dynamic_slice(total, (0, lax.rem(zl + k, 4) * span), (block, span))
        part = jnp.concatenate([part, sums], axis=0)
        parts.append(part if k == 0 else move(part, "zl", k))
    total = sum(p.astype(f32) for p in parts)
    along, inner, left_dot = unpack(total[block:].reshape(-1, many), few)
    total = total[:block].astype(bf16)

    inner = spread * inner
    dots = along + inner * jnp.repeat(left_dot, tokens)
    scale = 0.5 / jnp.sqrt(f32(D))
    score = jnp.mean(jnp.tanh(scale * dots).reshape(few, tokens), axis=1)
    score = joined(score, "zh", zh)
    labels = jnp.arange(population, dtype=jnp.int32)
    rival = jnp.sum(jnp.where(opponent[:, None] == labels[None, :], score[None, :], 0.0), axis=1)
    fitness = payoff * (score - rival)

    low, high = total[:, :rows], total[:, rows:]
    same = lax.ppermute(jnp.where(first, low, high), ("y", "c", "zl"), turned(0))
    cross = lax.ppermute(jnp.where(first, high, low), ("y", "c", "zl"), turned(1))
    total = jnp.where(
        first, jnp.concatenate([same, cross], 0), jnp.concatenate([cross, same], 0)
    ).astype(f32).T
    inner = lax.dynamic_slice(inner, (here * rows,), (rows,))
    lowrank = inner.reshape(members, tokens)[:, :, None] * left_cols[:, None, :]
    mixed = (total + lowrank.reshape(rows, cols)).astype(bf16)

    right_all = lax.all_gather(jnp.roll(rights, zh, axis=0), ("y", "c"), axis=0, tiled=False)
    scaled = lefts.reshape(4, 4, 2, members, 192)[..., :block].transpose(0, 2, 1, 3, 4).astype(f32)
    fitness = fitness.reshape(4, 4, 2, members).transpose(1, 2, 0, 3)
    scaled = (fitness[..., None] * scaled).astype(bf16).reshape(population, block)
    term = lax.dot_general(
        scaled, right_all.reshape(population, width), (((0,), (0,)), ((), ())),
        preferred_element_type=f32,
    )
    return mixed, term / jnp.sqrt(f32(population))


def solution(mesh):
    fine = Mesh(mesh.devices.reshape(SIZES), AXES)
    member, tensor = ("zh", "y", "c"), ("x", "zl")
    in_specs = (
        P(member, tensor), P(member, tensor), P(member, None), P(member, tensor), P(tensor), P(), P(),
    )
    out_specs = (P(member, tensor), P(member, tensor))
    return jax.shard_map(
        per_device, mesh=fine, in_specs=in_specs, out_specs=out_specs, check_vma=False
    )
```

```python
import jax
import jax.numpy as jnp
from jax import lax
from jax.sharding import Mesh, PartitionSpec as P

D = 5120
FF = 16384
AXES = ("zh", "y", "c", "x", "zl")
SIZES = (4, 4, 2, 4, 4)


def place(*index):
    at = 0
    for i, size in zip(index, SIZES):
        at = at * size + i
    return at


def ring(step):
    return [(i, (i + step) % 4) for i in range(4)]


def swapped(flip):
    return [
        (place(zh, y, c, x, zl), place(x, zl, c ^ flip, zh, y))
        for zh in range(4) for y in range(4) for c in range(2) for x in range(4) for zl in range(4)
    ]


def turned(flip):
    return [
        ((y * 2 + c) * 4 + zl, (zl * 2 + (c ^ flip)) * 4 + y)
        for y in range(4) for c in range(2) for zl in range(4)
    ]


def move(value, axis, step):
    return lax.ppermute(value, axis, ring(step))


def pairs(step):
    return [(i, i ^ step) for i in range(4)]


def joined(value, axis, index):
    for step, later in ((1, index % 2 == 1), (3, index >= 2)):
        got = lax.ppermute(value, axis, pairs(step))
        value = jnp.concatenate([jnp.where(later, got, value), jnp.where(later, value, got)], axis=0)
    return value


def in_three(value):
    terms = []
    for _ in range(3):
        term = lax.reduce_precision(value, 8, 7)
        terms.append(term.astype(jnp.bfloat16))
        value = value - term
    return jnp.stack(terms)


def placed(value, index, count):
    size = value.shape[0]
    return lax.dynamic_update_slice(jnp.zeros((size * count,), value.dtype), value, (index * size,))


def per_device(features, down_weight, member_left, member_right, probe, payoff, opponent):
    f32, bf16 = jnp.float32, jnp.bfloat16
    rows, width = features.shape
    members = member_right.shape[0]
    tokens = rows // members
    population = payoff.shape[0]
    block = down_weight.shape[0]
    cols = probe.shape[0]
    spread = 1.0 / jnp.sqrt(f32(FF))
    zh, y, c, x, zl = (lax.axis_index(a) for a in AXES)
    first = c == 0
    group = 8
    few, many = group * members, group * rows
    here = y * 2 + c

    gathered = lax.all_gather(features, ("y", "c"), axis=0, tiled=True)

    own = jnp.concatenate([down_weight, member_right], axis=0)
    cut = own.shape[0] // 2
    before = move(own, "zh", 1)
    after = move(own, "zh", -1)
    far = [move(before[:cut], "zh", 1), move(after[cut:], "zh", -1)]
    stack = jnp.concatenate([own, after] + far + [before], axis=0).reshape(4, *own.shape)
    weight, rights = stack[:, :block], stack[:, block:]

    probes = lax.psum(placed(probe, x, 4), "x").reshape(4, cols)
    probes = jnp.where(first, probes[:, :block], probes[:, block:])
    probes = lax.ppermute(probes, ("y", "c", "zl"), turned(0))

    left_cols = lax.dynamic_slice(member_left, (0, (x * 4 + zl) * cols), (members, cols))
    mine = jnp.where(first, left_cols[:, :block], left_cols[:, block:])
    other = jnp.where(first, left_cols[:, block:], left_cols[:, :block])
    mine = lax.ppermute(mine, AXES, swapped(0))
    other = lax.ppermute(other, AXES, swapped(1))
    lefts = jnp.where(first, jnp.concatenate([mine, other], 0), jnp.concatenate([other, mine], 0))
    lefts = jnp.pad(lefts, ((0, 0), (0, 192 - block))).reshape(8, many)
    left_cols = left_cols.astype(f32)

    part = lax.dot_general(
        weight.reshape(-1, width), gathered, (((1,), (1,)), ((), ())), preferred_element_type=f32
    ).astype(bf16).reshape(4, block, many)
    parts = []
    for k in range(4):
        one = lax.dynamic_index_in_dim(part, lax.rem(x + k + 4 - zh, 4), 0, keepdims=False)
        one = jnp.concatenate([one, lefts], axis=0)
        parts.append(one if k == 0 else move(one, "x", k))
    total = sum(p[:block].astype(f32) for p in parts).astype(bf16)
    lefts = jnp.stack([parts[k][block:] for k in (0, 3, 2, 1)])
    lefts, total = lax.optimization_barrier((lefts, total))
    lefts = joined(jnp.roll(lefts, x, axis=0).reshape(-1, many), "zl", zl)

    probes = in_three(jnp.roll(probes, -zh, axis=0)).reshape(3, -1)
    direction = lax.dot_general(
        probes, weight.reshape(-1, width), (((1,), (0,)), ((), ())), preferred_element_type=f32
    ).sum(0)
    along = lax.dot_general(
        in_three(direction), gathered, (((1,), (1,)), ((), ())), preferred_element_type=f32
    ).sum(0)
    inner = jnp.sum(
        features.astype(f32).reshape(members, tokens, width) * member_right.astype(f32)[:, None, :],
        axis=2,
    ).reshape(rows)
    left_dot = jnp.sum(left_cols * probe[None, :], axis=1)
    sums = jnp.concatenate([along, placed(inner, here, group), placed(left_dot, here, group)])
    for axis in ("c", "y", "x", "zl"):
        sums = lax.psum(sums, axis)
    along, inner, left_dot = jnp.split(sums, [many, 2 * many])
    inner = spread * inner
    dots = along + inner * jnp.repeat(left_dot, tokens)
    scale = 0.5 / jnp.sqrt(f32(D))
    score = jnp.mean(jnp.tanh(scale * dots).reshape(few, tokens), axis=1)
    score = lax.psum(placed(score, zh, 4), "zh")
    labels = jnp.arange(population, dtype=jnp.int32)
    rival = jnp.sum(jnp.where(opponent[:, None] == labels[None, :], score[None, :], 0.0), axis=1)
    fitness = payoff * (score - rival)

    span = 2 * rows
    parts = []
    for k in range(4):
        part = lax.dynamic_slice(total, (0, lax.rem(zl + k, 4) * span), (block, span))
        parts.append(part if k == 0 else move(part, "zl", k))
    total = sum(p.astype(f32) for p in parts).astype(bf16)

    low, high = total[:, :rows], total[:, rows:]
    same = lax.ppermute(jnp.where(first, low, high), ("y", "c", "zl"), turned(0))
    cross = lax.ppermute(jnp.where(first, high, low), ("y", "c", "zl"), turned(1))
    total = jnp.where(
        first, jnp.concatenate([same, cross], 0), jnp.concatenate([cross, same], 0)
    ).astype(f32).T
    inner = lax.dynamic_slice(inner, (here * rows,), (rows,))
    lowrank = inner.reshape(members, tokens)[:, :, None] * left_cols[:, None, :]
    mixed = (total + lowrank.reshape(rows, cols)).astype(bf16)

    right_all = lax.all_gather(jnp.roll(rights, zh, axis=0), ("y", "c"), axis=0, tiled=False)
    scaled = lefts.reshape(4, 4, 2, members, 192)[..., :block].transpose(0, 2, 1, 3, 4).astype(f32)
    fitness = fitness.reshape(4, 4, 2, members).transpose(1, 2, 0, 3)
    scaled = (fitness[..., None] * scaled).astype(bf16).reshape(population, block)
    term = lax.dot_general(
        scaled, right_all.reshape(population, width), (((0,), (0,)), ((), ())),
        preferred_element_type=f32,
    )
    return mixed, term / jnp.sqrt(f32(population))


def solution(mesh):
    fine = Mesh(mesh.devices.reshape(SIZES), AXES)
    member, tensor = ("zh", "y", "c"), ("x", "zl")
    in_specs = (
        P(member, tensor), P(member, tensor), P(member, None), P(member, tensor), P(tensor), P(), P(),
    )
    out_specs = (P(member, tensor), P(member, tensor))
    return jax.shard_map(
        per_device, mesh=fine, in_specs=in_specs, out_specs=out_specs, check_vma=False
    )
```

```python
import jax
import jax.numpy as jnp
from jax import lax
from jax.sharding import Mesh, PartitionSpec as P

D = 5120
FF = 16384
AXES = ("zh", "y", "c", "x", "zl")
SIZES = (4, 4, 2, 4, 4)


def place(*index):
    at = 0
    for i, size in zip(index, SIZES):
        at = at * size + i
    return at


def ring(step):
    return [(i, (i + step) % 4) for i in range(4)]


def swapped(flip):
    return [
        (place(zh, y, c, x, zl), place(x, zl, c ^ flip, zh, y))
        for zh in range(4) for y in range(4) for c in range(2) for x in range(4) for zl in range(4)
    ]


def turned(flip):
    return [
        ((y * 2 + c) * 4 + zl, (zl * 2 + (c ^ flip)) * 4 + y)
        for y in range(4) for c in range(2) for zl in range(4)
    ]


def move(value, axis, step):
    return lax.ppermute(value, axis, ring(step))


def pairs(step):
    return [(i, i ^ step) for i in range(4)]


def joined(value, axis, index):
    for step, later in ((1, index % 2 == 1), (3, index >= 2)):
        got = lax.ppermute(value, axis, pairs(step))
        value = jnp.concatenate([jnp.where(later, got, value), jnp.where(later, value, got)], axis=0)
    return value


def in_three(value):
    terms = []
    for _ in range(3):
        term = lax.reduce_precision(value, 8, 7)
        terms.append(term.astype(jnp.bfloat16))
        value = value - term
    return jnp.stack(terms)


def placed(value, index, count):
    size = value.shape[0]
    return lax.dynamic_update_slice(jnp.zeros((size * count,), value.dtype), value, (index * size,))


def per_device(features, down_weight, member_left, member_right, probe, payoff, opponent):
    f32, bf16 = jnp.float32, jnp.bfloat16
    rows, width = features.shape
    members = member_right.shape[0]
    tokens = rows // members
    population = payoff.shape[0]
    block = down_weight.shape[0]
    cols = probe.shape[0]
    spread = 1.0 / jnp.sqrt(f32(FF))
    zh, y, c, x, zl = (lax.axis_index(a) for a in AXES)
    first = c == 0
    group = 8
    few, many = group * members, group * rows
    here = y * 2 + c

    gathered = lax.all_gather(features, ("y", "c"), axis=0, tiled=True)

    left_cols = lax.dynamic_slice(member_left, (0, (x * 4 + zl) * cols), (members, cols)).astype(f32)
    payload = jnp.concatenate([left_cols, probe[None, :]], axis=0)
    mine = jnp.where(first, payload[:, :block], payload[:, block:])
    other = jnp.where(first, left_cols[:, block:], left_cols[:, :block])
    mine = lax.ppermute(mine, AXES, swapped(0))
    other = lax.ppermute(other, AXES, swapped(1))

    lead = 96
    chunks = [down_weight[:lead], jnp.concatenate([down_weight[lead:], member_right], axis=0)]
    chunks[1], mine, other = lax.optimization_barrier((chunks[1], mine, other))
    cut = lead // 2
    steps = [(move(own, "zh", 1), move(own, "zh", -1)) for own in chunks]

    direction = jnp.sum(down_weight.astype(f32) * mine[members][:, None], axis=0)
    inner = jnp.sum(
        features.astype(f32).reshape(members, tokens, width) * member_right.astype(f32)[:, None, :],
        axis=2,
    ).reshape(rows)
    left_dot = jnp.sum(left_cols * probe[None, :], axis=1)
    early = jnp.concatenate([direction, placed(inner, here, group), placed(left_dot, here, group)])
    early = lax.psum(lax.psum(early, "c"), "y")

    direction = jnp.pad(in_three(early[:width]), ((0, 5), (0, 0)))
    (before, after), (before_two, after_two) = steps
    low = move(jnp.concatenate([before[:cut], direction], axis=0), "zh", 1)
    high = move(jnp.concatenate([after[cut:], direction], axis=0), "zh", -1)
    low_two = move(jnp.concatenate([before_two[:cut], low[cut:]], axis=0), "zh", 1)
    high_two = move(after_two[cut:], "zh", -1)
    direction = sum(d.astype(f32) for d in (direction, low[cut:], high[cut:], low_two[cut:])).sum(0)
    stacks = [
        jnp.concatenate([own, late, one[:cut], two, soon], axis=0).reshape(4, lead, width)
        for own, late, one, two, soon in (
            (chunks[0], after, low, high[: lead - cut], before),
            (chunks[1], after_two, low_two, high_two, before_two),
        )
    ]
    rest = block - lead
    weights, rights = [stacks[0], stacks[1][:, :rest]], stacks[1][:, rest:]

    mine = mine[:members]
    lefts = jnp.where(first, jnp.concatenate([mine, other], 0), jnp.concatenate([other, mine], 0))
    lefts = jnp.pad(lefts.astype(bf16), ((0, 0), (0, 192 - block))).reshape(8, many)

    def products(weight):
        part = lax.dot_general(
            weight.reshape(-1, width), gathered, (((1,), (1,)), ((), ())),
            preferred_element_type=f32,
        ).astype(bf16).reshape(4, -1, many)
        return [
            lax.dynamic_index_in_dim(part, lax.rem(x + k + 4 - zh, 4), 0, keepdims=False)
            for k in range(4)
        ]

    ones = [jnp.concatenate([p, lefts], axis=0) for p in products(weights[0])]
    ones = [ones[0]] + [move(ones[k], "x", k) for k in (1, 2, 3)]
    weights[1], direction, ones[1] = lax.optimization_barrier((weights[1], direction, ones[1]))

    along = lax.dot_general(
        in_three(direction), gathered, (((1,), (1,)), ((), ())), preferred_element_type=f32
    ).sum(0)
    sums = lax.psum(jnp.concatenate([along, early[width:]]), "x")

    twos = products(weights[1])
    twos, sums = lax.optimization_barrier((twos, sums))
    twos = [twos[0]] + [move(twos[k], "x", k) for k in (1, 2, 3)]
    sums, twos[1] = lax.optimization_barrier((sums, twos[1]))
    sums = lax.psum(sums, "zl")
    total = jnp.concatenate([
        sum(p[:lead].astype(f32) for p in ones).astype(bf16),
        sum(p.astype(f32) for p in twos).astype(bf16),
    ], axis=0)
    lefts = jnp.stack([ones[k][lead:] for k in (0, 3, 2, 1)])
    lefts, total = lax.optimization_barrier((lefts, total))
    lefts = joined(jnp.roll(lefts, x, axis=0).reshape(-1, many), "zl", zl)

    span = 2 * rows
    parts = []
    for k in range(4):
        part = lax.dynamic_slice(total, (0, lax.rem(zl + k, 4) * span), (block, span))
        parts.append(part if k == 0 else move(part, "zl", k))
    sums, parts[1] = lax.optimization_barrier((sums, parts[1]))
    total = sum(p.astype(f32) for p in parts).astype(bf16)

    along, inner, left_dot = jnp.split(sums, [many, 2 * many])
    inner = spread * inner
    dots = along + inner * jnp.repeat(left_dot, tokens)
    scale = 0.5 / jnp.sqrt(f32(D))
    score = jnp.mean(jnp.tanh(scale * dots).reshape(few, tokens), axis=1)
    score = lax.psum(placed(score, zh, 4), "zh")
    labels = jnp.arange(population, dtype=jnp.int32)
    rival = jnp.sum(jnp.where(opponent[:, None] == labels[None, :], score[None, :], 0.0), axis=1)
    fitness = payoff * (score - rival)

    low, high = total[:, :rows], total[:, rows:]
    same = lax.ppermute(jnp.where(first, low, high), ("y", "c", "zl"), turned(0))
    cross = lax.ppermute(jnp.where(first, high, low), ("y", "c", "zl"), turned(1))
    total = jnp.where(
        first, jnp.concatenate([same, cross], 0), jnp.concatenate([cross, same], 0)
    ).astype(f32).T
    inner = lax.dynamic_slice(inner, (here * rows,), (rows,))
    lowrank = inner.reshape(members, tokens)[:, :, None] * left_cols[:, None, :]
    mixed = (total + lowrank.reshape(rows, cols)).astype(bf16)

    right_all = lax.all_gather(jnp.roll(rights, zh, axis=0), ("y", "c"), axis=0, tiled=False)
    scaled = lefts.reshape(4, 4, 2, members, 192)[..., :block].transpose(0, 2, 1, 3, 4).astype(f32)
    fitness = fitness.reshape(4, 4, 2, members).transpose(1, 2, 0, 3)
    scaled = (fitness[..., None] * scaled).astype(bf16).reshape(population, block)
    term = lax.dot_general(
        scaled, right_all.reshape(population, width), (((0,), (0,)), ((), ())),
        preferred_element_type=f32,
    )
    return mixed, term / jnp.sqrt(f32(population))


def solution(mesh):
    fine = Mesh(mesh.devices.reshape(SIZES), AXES)
    member, tensor = ("zh", "y", "c"), ("x", "zl")
    in_specs = (
        P(member, tensor), P(member, tensor), P(member, None), P(member, tensor), P(tensor), P(), P(),
    )
    out_specs = (P(member, tensor), P(member, tensor))
    return jax.shard_map(
        per_device, mesh=fine, in_specs=in_specs, out_specs=out_specs, check_vma=False
    )
```

```python
import jax
import jax.numpy as jnp
from jax import lax
from jax.sharding import Mesh, PartitionSpec as P

D = 5120
FF = 16384
AXES = ("zh", "y", "c", "x", "zl")
SIZES = (4, 4, 2, 4, 4)


def place(*index):
    at = 0
    for i, size in zip(index, SIZES):
        at = at * size + i
    return at


def ring(step):
    return [(i, (i + step) % 4) for i in range(4)]


def swapped(flip):
    return [
        (place(zh, y, c, x, zl), place(x, zl, c ^ flip, zh, y))
        for zh in range(4) for y in range(4) for c in range(2) for x in range(4) for zl in range(4)
    ]


def turned():
    return [(y * 4 + zl, zl * 4 + y) for y in range(4) for zl in range(4)]


def move(value, axis, step):
    return lax.ppermute(value, axis, ring(step))


def pairs(step):
    return [(i, i ^ step) for i in range(4)]


def joined(value, axis, index):
    for step, later in ((1, index % 2 == 1), (3, index >= 2)):
        got = lax.ppermute(value, axis, pairs(step))
        value = jnp.concatenate([jnp.where(later, got, value), jnp.where(later, value, got)], axis=0)
    return value


def placed(value, index, count):
    size = value.shape[0]
    return lax.dynamic_update_slice(jnp.zeros((size * count,), value.dtype), value, (index * size,))


def per_device(features, down_weight, member_left, member_right, probe, payoff, opponent):
    f32, bf16 = jnp.float32, jnp.bfloat16
    rows, width = features.shape
    members = member_right.shape[0]
    tokens = rows // members
    population = payoff.shape[0]
    block = down_weight.shape[0]
    cols = probe.shape[0]
    spread = 1.0 / jnp.sqrt(f32(FF))
    zh, y, c, x, zl = (lax.axis_index(a) for a in AXES)
    first = c == 0
    here = y * 2 + c

    own = jnp.concatenate([down_weight, member_right], axis=0)
    stack = lax.all_gather(own, ("zh", "c"), axis=0, tiled=True).reshape(4, 2, -1, width)
    weight = stack[:, :, :block].reshape(-1, width)
    rights = lax.all_gather(stack[:, :, block:], "y", axis=0, tiled=False)

    around = [features] + [move(features, "y", -j) for j in (1, 2, 3)]

    left_cols = lax.dynamic_slice(member_left, (0, (x * 4 + zl) * cols), (members, cols)).astype(f32)
    payload = jnp.concatenate([left_cols, probe[None, :]], axis=0)
    mine = jnp.where(first, payload[:, :block], payload[:, block:])
    other = jnp.where(first, left_cols[:, block:], left_cols[:, :block])
    mine = lax.ppermute(mine, AXES, swapped(0))
    other = lax.ppermute(other, AXES, swapped(1))

    direction = jnp.sum(down_weight.astype(f32) * mine[members][:, None], axis=0)
    direction = lax.psum(lax.psum(direction, ("y", "c")), "zh")
    wide = features.astype(f32)
    along = jnp.sum(wide * direction[None, :], axis=1)
    inner = jnp.sum(
        wide.reshape(members, tokens, width) * member_right.astype(f32)[:, None, :], axis=2
    ).reshape(rows)
    left_dot = jnp.sum(left_cols * probe[None, :], axis=1)
    sums = lax.psum(lax.psum(jnp.concatenate([along, inner, left_dot]), "x"), "zl")
    along, inner, left_dot = jnp.split(sums, [rows, 2 * rows])
    inner = spread * inner
    dots = along + inner * jnp.repeat(left_dot, tokens)
    scale = 0.5 / jnp.sqrt(f32(D))
    own_score = jnp.mean(jnp.tanh(scale * dots).reshape(members, tokens), axis=1)

    many = 4 * rows
    mine = mine[:members]
    lefts = jnp.where(first, jnp.concatenate([mine, other], 0), jnp.concatenate([other, mine], 0))
    lefts = jnp.pad(lefts.astype(bf16), ((0, 0), (0, 192 - block))).reshape(-1, many)
    part = lax.dot_general(
        weight, jnp.concatenate(around, axis=0), (((1,), (1,)), ((), ())),
        preferred_element_type=f32,
    ).astype(bf16).reshape(4, cols, many)
    parts = []
    for k in range(4):
        one = lax.dynamic_index_in_dim(part, lax.rem(x + k, 4), 0, keepdims=False)
        one = jnp.concatenate([one, lefts], axis=0)
        parts.append(one if k == 0 else move(one, "x", k))
    own_score, parts[1] = lax.optimization_barrier((own_score, parts[1]))
    score = lax.psum(placed(own_score, here, 8), ("y", "c"))
    total = sum(p[:cols].astype(f32) for p in parts).astype(bf16)
    lefts = jnp.stack([parts[k][cols:] for k in (0, 3, 2, 1)])
    lefts, total = lax.optimization_barrier((lefts, total))
    lefts = joined(jnp.roll(lefts, x, axis=0).reshape(-1, many), "zl", zl)

    total = total.T.reshape(4, rows, cols)
    parts = []
    for k in range(4):
        one = lax.dynamic_index_in_dim(total, lax.rem(zl + k + 4 - y, 4), 0, keepdims=False)
        parts.append(one if k == 0 else move(one, "zl", k))
    score, parts[1] = lax.optimization_barrier((score, parts[1]))
    score = lax.psum(placed(score, zh, 4), "zh")
    total = sum(p.astype(f32) for p in parts).astype(bf16)

    total = lax.ppermute(total, ("y", "zl"), turned()).astype(f32)
    lowrank = inner.reshape(members, tokens)[:, :, None] * left_cols[:, None, :]
    mixed = (total + lowrank.reshape(rows, cols)).astype(bf16)

    labels = jnp.arange(population, dtype=jnp.int32)
    rival = jnp.sum(jnp.where(opponent[:, None] == labels[None, :], score[None, :], 0.0), axis=1)
    fitness = payoff * (score - rival)
    fitness = fitness.reshape(4, 4, -1).transpose(1, 0, 2).reshape(population, 1)
    scaled = lefts.reshape(population, 192)[:, :block].astype(f32)
    scaled = (fitness * scaled).astype(bf16)
    term = lax.dot_general(
        scaled, rights.reshape(population, width), (((0,), (0,)), ((), ())),
        preferred_element_type=f32,
    )
    return mixed, term / jnp.sqrt(f32(population))


def solution(mesh):
    fine = Mesh(mesh.devices.reshape(SIZES), AXES)
    member, tensor = ("zh", "y", "c"), ("x", "zl")
    in_specs = (
        P(member, tensor), P(member, tensor), P(member, None), P(member, tensor), P(tensor), P(), P(),
    )
    out_specs = (P(member, tensor), P(member, tensor))
    return jax.shard_map(
        per_device, mesh=fine, in_specs=in_specs, out_specs=out_specs, check_vma=False
    )
```

```python
import jax
import jax.numpy as jnp
from jax import lax
from jax.sharding import Mesh, PartitionSpec as P

D = 5120
FF = 16384
AXES = ("zh", "y", "c", "x", "zl")
SIZES = (4, 4, 2, 4, 4)


def place(*index):
    at = 0
    for i, size in zip(index, SIZES):
        at = at * size + i
    return at


def ring(step):
    return [(i, (i + step) % 4) for i in range(4)]


def swapped(flip):
    return [
        (place(zh, y, c, x, zl), place(x, zl, c ^ flip, zh, y))
        for zh in range(4) for y in range(4) for c in range(2) for x in range(4) for zl in range(4)
    ]


def turned():
    return [(y * 4 + zl, zl * 4 + y) for y in range(4) for zl in range(4)]


def move(value, axis, step):
    return lax.ppermute(value, axis, ring(step))


def pairs(step):
    return [(i, i ^ step) for i in range(4)]


def joined(value, axis, index):
    for step, later in ((1, index % 2 == 1), (3, index >= 2)):
        got = lax.ppermute(value, axis, pairs(step))
        value = jnp.concatenate([jnp.where(later, got, value), jnp.where(later, value, got)], axis=0)
    return value


def placed(value, index, count):
    size = value.shape[0]
    return lax.dynamic_update_slice(jnp.zeros((size * count,), value.dtype), value, (index * size,))


def per_device(features, down_weight, member_left, member_right, probe, payoff, opponent):
    f32, bf16 = jnp.float32, jnp.bfloat16
    rows, width = features.shape
    members = member_right.shape[0]
    tokens = rows // members
    population = payoff.shape[0]
    block = down_weight.shape[0]
    cols = probe.shape[0]
    spread = 1.0 / jnp.sqrt(f32(FF))
    zh, y, c, x, zl = (lax.axis_index(a) for a in AXES)
    first = c == 0
    here = y * 2 + c

    own = jnp.concatenate([down_weight, member_right], axis=0)
    stack = lax.all_gather(own, ("zh", "c"), axis=0, tiled=True).reshape(4, 2, -1, width)
    weight = stack[:, :, :block].reshape(-1, width)
    rights = lax.all_gather(stack[:, :, block:], "y", axis=0, tiled=False)

    level = jnp.where(first, probe[:block], probe[block:])
    level = lax.ppermute(level, AXES, swapped(0))
    direction = jnp.sum(down_weight.astype(f32) * level[:, None], axis=0)
    direction = lax.psum(direction, ("y", "c"))

    features, member_left, direction = lax.optimization_barrier((features, member_left, direction))
    around = [features] + [move(features, "y", -j) for j in (1, 2, 3)]

    left_cols = lax.dynamic_slice(member_left, (0, (x * 4 + zl) * cols), (members, cols))
    mine = jnp.where(first, left_cols[:, :block], left_cols[:, block:])
    other = jnp.where(first, left_cols[:, block:], left_cols[:, :block])
    mine = lax.ppermute(mine, AXES, swapped(0))
    other = lax.ppermute(other, AXES, swapped(1))
    left_cols = left_cols.astype(f32)

    direction = lax.psum(direction, "zh")
    wide = features.astype(f32)
    along = jnp.sum(wide * direction[None, :], axis=1)
    inner = jnp.sum(
        wide.reshape(members, tokens, width) * member_right.astype(f32)[:, None, :], axis=2
    ).reshape(rows)
    left_dot = jnp.sum(left_cols * probe[None, :], axis=1)
    sums = lax.psum(lax.psum(jnp.concatenate([along, inner, left_dot]), "x"), "zl")
    along, inner, left_dot = jnp.split(sums, [rows, 2 * rows])
    inner = spread * inner
    dots = along + inner * jnp.repeat(left_dot, tokens)
    scale = 0.5 / jnp.sqrt(f32(D))
    score = jnp.mean(jnp.tanh(scale * dots).reshape(members, tokens), axis=1)
    score = lax.psum(placed(score, here, 8), ("y", "c"))

    many = 4 * rows
    lefts = jnp.where(first, jnp.concatenate([mine, other], 0), jnp.concatenate([other, mine], 0))
    lefts = jnp.pad(lefts, ((0, 0), (0, 192 - block))).reshape(-1, many)
    part = lax.dot_general(
        weight, jnp.concatenate(around, axis=0), (((1,), (1,)), ((), ())),
        preferred_element_type=f32,
    ).astype(bf16).reshape(4, cols, many)
    parts = []
    for k in range(4):
        one = lax.dynamic_index_in_dim(part, lax.rem(x + k, 4), 0, keepdims=False)
        one = jnp.concatenate([one, lefts], axis=0)
        parts.append(one if k == 0 else move(one, "x", k))
    score, parts[1] = lax.optimization_barrier((score, parts[1]))
    score = lax.psum(placed(score, zh, 4), "zh")
    total = sum(p[:cols].astype(f32) for p in parts).astype(bf16)
    lefts = jnp.stack([parts[k][cols:] for k in (0, 3, 2, 1)])
    lefts, total = lax.optimization_barrier((lefts, total))
    lefts = joined(jnp.roll(lefts, x, axis=0).reshape(-1, many), "zl", zl)

    total = total.T.reshape(4, rows, cols)
    parts = []
    for k in range(4):
        one = lax.dynamic_index_in_dim(total, lax.rem(zl + k + 4 - y, 4), 0, keepdims=False)
        parts.append(one if k == 0 else move(one, "zl", k))
    total = sum(p.astype(f32) for p in parts).astype(bf16)

    total = lax.ppermute(total, ("y", "zl"), turned()).astype(f32)
    lowrank = inner.reshape(members, tokens)[:, :, None] * left_cols[:, None, :]
    mixed = (total + lowrank.reshape(rows, cols)).astype(bf16)

    labels = jnp.arange(population, dtype=jnp.int32)
    rival = jnp.sum(jnp.where(opponent[:, None] == labels[None, :], score[None, :], 0.0), axis=1)
    fitness = payoff * (score - rival)
    fitness = fitness.reshape(4, 4, -1).transpose(1, 0, 2).reshape(population, 1)
    scaled = lefts.reshape(population, 192)[:, :block].astype(f32)
    scaled = (fitness * scaled).astype(bf16)
    term = lax.dot_general(
        scaled, rights.reshape(population, width), (((0,), (0,)), ((), ())),
        preferred_element_type=f32,
    )
    return mixed, term / jnp.sqrt(f32(population))


def solution(mesh):
    fine = Mesh(mesh.devices.reshape(SIZES), AXES)
    member, tensor = ("zh", "y", "c"), ("x", "zl")
    in_specs = (
        P(member, tensor), P(member, tensor), P(member, None), P(member, tensor), P(tensor), P(), P(),
    )
    out_specs = (P(member, tensor), P(member, tensor))
    return jax.shard_map(
        per_device, mesh=fine, in_specs=in_specs, out_specs=out_specs, check_vma=False
    )
```

```python
import jax
import jax.numpy as jnp
from jax import lax
from jax.sharding import Mesh, PartitionSpec as P

D = 5120
FF = 16384
AXES = ("zh", "y", "c", "x", "zl")
SIZES = (4, 4, 2, 4, 4)


def place(*index):
    at = 0
    for i, size in zip(index, SIZES):
        at = at * size + i
    return at


def ring(step):
    return [(i, (i + step) % 4) for i in range(4)]


def swapped(flip):
    return [
        (place(zh, y, c, x, zl), place(x, zl, c ^ flip, zh, y))
        for zh in range(4) for y in range(4) for c in range(2) for x in range(4) for zl in range(4)
    ]


def turned():
    return [(y * 4 + zl, zl * 4 + y) for y in range(4) for zl in range(4)]


def move(value, axis, step):
    return lax.ppermute(value, axis, ring(step))


def pairs(step):
    return [(i, i ^ step) for i in range(4)]


def joined(value, axis, index):
    for step, later in ((1, index % 2 == 1), (3, index >= 2)):
        got = lax.ppermute(value, axis, pairs(step))
        value = jnp.concatenate([jnp.where(later, got, value), jnp.where(later, value, got)], axis=0)
    return value


def placed(value, index, count):
    size = value.shape[0]
    return lax.dynamic_update_slice(jnp.zeros((size * count,), value.dtype), value, (index * size,))


def per_device(features, down_weight, member_left, member_right, probe, payoff, opponent):
    f32, bf16 = jnp.float32, jnp.bfloat16
    rows, width = features.shape
    members = member_right.shape[0]
    tokens = rows // members
    population = payoff.shape[0]
    block = down_weight.shape[0]
    cols = probe.shape[0]
    spread = 1.0 / jnp.sqrt(f32(FF))
    zh, y, c, x, zl = (lax.axis_index(a) for a in AXES)
    first = c == 0
    here = y * 2 + c

    own = jnp.concatenate([down_weight, member_right], axis=0)
    stack = lax.all_gather(own, ("zh", "c"), axis=0, tiled=True).reshape(4, 2, -1, width)
    weight = stack[:, :, :block].reshape(-1, width)
    rights = lax.all_gather(stack[:, :, block:], "y", axis=0, tiled=False)

    left_cols = lax.dynamic_slice(member_left, (0, (x * 4 + zl) * cols), (members, cols)).astype(f32)
    payload = jnp.concatenate([left_cols, probe[None, :]], axis=0)
    mine = jnp.where(first, payload[:, :block], payload[:, block:])
    other = jnp.where(first, left_cols[:, block:], left_cols[:, :block])
    mine = lax.ppermute(mine, AXES, swapped(0))
    other = lax.ppermute(other, AXES, swapped(1))
    mine, other = lax.optimization_barrier((mine, other))

    direction = jnp.sum(down_weight.astype(f32) * mine[members][:, None], axis=0)
    direction = lax.psum(direction, ("y", "c"))

    features, direction = lax.optimization_barrier((features, direction))
    around = [features] + [move(features, "y", -j) for j in (1, 2, 3)]

    direction = lax.psum(direction, "zh")
    wide = features.astype(f32)
    along = jnp.sum(wide * direction[None, :], axis=1)
    inner = jnp.sum(
        wide.reshape(members, tokens, width) * member_right.astype(f32)[:, None, :], axis=2
    ).reshape(rows)
    left_dot = jnp.sum(left_cols * probe[None, :], axis=1)
    sums = lax.psum(lax.psum(jnp.concatenate([along, inner, left_dot]), "x"), "zl")
    along, inner, left_dot = jnp.split(sums, [rows, 2 * rows])
    inner = spread * inner
    dots = along + inner * jnp.repeat(left_dot, tokens)
    scale = 0.5 / jnp.sqrt(f32(D))
    score = jnp.mean(jnp.tanh(scale * dots).reshape(members, tokens), axis=1)
    score = lax.psum(placed(score, here, 8), ("y", "c"))

    many = 4 * rows
    mine = mine[:members]
    lefts = jnp.where(first, jnp.concatenate([mine, other], 0), jnp.concatenate([other, mine], 0))
    lefts = jnp.pad(lefts.astype(bf16), ((0, 0), (0, 192 - block))).reshape(-1, many)
    part = lax.dot_general(
        weight, jnp.concatenate(around, axis=0), (((1,), (1,)), ((), ())),
        preferred_element_type=f32,
    ).astype(bf16).reshape(4, cols, many)
    parts = []
    for k in range(4):
        one = lax.dynamic_index_in_dim(part, lax.rem(x + k, 4), 0, keepdims=False)
        one = jnp.concatenate([one, lefts], axis=0)
        parts.append(one if k == 0 else move(one, "x", k))
    score, parts[1] = lax.optimization_barrier((score, parts[1]))
    score = lax.psum(placed(score, zh, 4), "zh")
    total = sum(p[:cols].astype(f32) for p in parts).astype(bf16)
    lefts = jnp.stack([parts[k][cols:] for k in (0, 3, 2, 1)])
    lefts, total, score = lax.optimization_barrier((lefts, total, score))
    lefts = joined(jnp.roll(lefts, x, axis=0).reshape(-1, many), "zl", zl)

    total = total.T.reshape(4, rows, cols)
    parts = []
    for k in range(4):
        one = lax.dynamic_index_in_dim(total, lax.rem(zl + k + 4 - y, 4), 0, keepdims=False)
        parts.append(one if k == 0 else move(one, "zl", k))
    total = sum(p.astype(f32) for p in parts).astype(bf16)

    total = lax.ppermute(total, ("y", "zl"), turned()).astype(f32)
    lowrank = inner.reshape(members, tokens)[:, :, None] * left_cols[:, None, :]
    mixed = (total + lowrank.reshape(rows, cols)).astype(bf16)

    labels = jnp.arange(population, dtype=jnp.int32)
    rival = jnp.sum(jnp.where(opponent[:, None] == labels[None, :], score[None, :], 0.0), axis=1)
    fitness = payoff * (score - rival)
    fitness = fitness.reshape(4, 4, -1).transpose(1, 0, 2).reshape(population, 1)
    scaled = lefts.reshape(population, 192)[:, :block].astype(f32)
    scaled = (fitness * scaled).astype(bf16)
    term = lax.dot_general(
        scaled, rights.reshape(population, width), (((0,), (0,)), ((), ())),
        preferred_element_type=f32,
    )
    return mixed, term / jnp.sqrt(f32(population))


def solution(mesh):
    fine = Mesh(mesh.devices.reshape(SIZES), AXES)
    member, tensor = ("zh", "y", "c"), ("x", "zl")
    in_specs = (
        P(member, tensor), P(member, tensor), P(member, None), P(member, tensor), P(tensor), P(), P(),
    )
    out_specs = (P(member, tensor), P(member, tensor))
    return jax.shard_map(
        per_device, mesh=fine, in_specs=in_specs, out_specs=out_specs, check_vma=False
    )
```

```python
import jax
import jax.numpy as jnp
from jax import lax
from jax.sharding import Mesh, PartitionSpec as P

D = 5120
FF = 16384
AXES = ("zh", "y", "c", "x", "zl")
SIZES = (4, 4, 2, 4, 4)


def place(*index):
    at = 0
    for i, size in zip(index, SIZES):
        at = at * size + i
    return at


def ring(step):
    return [(i, (i + step) % 4) for i in range(4)]


def swapped():
    return [
        (place(zh, y, c, x, zl), place(x, zl, c, zh, y))
        for zh in range(4) for y in range(4) for c in range(2) for x in range(4) for zl in range(4)
    ]


def turned():
    return [(y * 4 + zl, zl * 4 + y) for y in range(4) for zl in range(4)]


def move(value, axis, step):
    return lax.ppermute(value, axis, ring(step))


def pairs(step):
    return [(i, i ^ step) for i in range(4)]


def joined(value, axis, index):
    for step, later in ((1, index % 2 == 1), (3, index >= 2)):
        got = lax.ppermute(value, axis, pairs(step))
        value = jnp.concatenate([jnp.where(later, got, value), jnp.where(later, value, got)], axis=0)
    return value


def in_three(value):
    terms = []
    for _ in range(3):
        term = lax.reduce_precision(value, 8, 7)
        terms.append(term.astype(jnp.bfloat16))
        value = value - term
    return jnp.stack(terms)


def placed(value, index, count):
    size = value.shape[0]
    return lax.dynamic_update_slice(jnp.zeros((size * count,), value.dtype), value, (index * size,))


def per_device(features, down_weight, member_left, member_right, probe, payoff, opponent):
    f32, bf16 = jnp.float32, jnp.bfloat16
    rows, width = features.shape
    members = member_right.shape[0]
    tokens = rows // members
    population = payoff.shape[0]
    block = down_weight.shape[0]
    cols = probe.shape[0]
    spread = 1.0 / jnp.sqrt(f32(FF))
    zh, y, c, x, zl = (lax.axis_index(a) for a in AXES)
    first = c == 0
    many = 4 * rows

    weight = lax.all_gather(down_weight, ("zh", "c"), axis=0, tiled=True)

    around = [features] + [move(features, "y", -j) for j in (1, 2, 3)]
    around = jnp.concatenate(around, axis=0)

    cut = members // 2
    before = move(member_right, "zh", 1)
    after = move(member_right, "zh", -1)
    far = [move(before[:cut], "zh", 1), move(after[cut:], "zh", -1)]
    rights = jnp.concatenate([member_right, after] + far + [before], axis=0)
    rights = jnp.roll(rights.reshape(4, members, width), zh, axis=0)
    rights = lax.all_gather(rights, ("y", "c"), axis=0, tiled=False)

    probes = lax.psum(placed(probe, x, 4), "x")
    probes = lax.ppermute(probes, ("y", "zl"), turned())

    left_cols = lax.dynamic_slice(member_left, (0, (x * 4 + zl) * cols), (members, cols))
    lefts = lax.ppermute(left_cols, AXES, swapped())
    mine = jnp.where(first, lefts[:, :block], lefts[:, block:])
    other = jnp.where(first, lefts[:, block:], lefts[:, :block])
    other = lax.ppermute(other, "c", [(0, 1), (1, 0)])
    lefts = jnp.where(first, jnp.concatenate([mine, other], 0), jnp.concatenate([other, mine], 0))
    lefts = jnp.pad(lefts, ((0, 0), (0, 192 - block))).reshape(-1, many)
    left_cols = left_cols.astype(f32)

    part = lax.dot_general(
        weight, around, (((1,), (1,)), ((), ())), preferred_element_type=f32
    ).astype(bf16).reshape(4, cols, many)
    parts = []
    for k in range(4):
        one = lax.dynamic_index_in_dim(part, lax.rem(x + k, 4), 0, keepdims=False)
        one = jnp.concatenate([one, lefts], axis=0)
        parts.append(one if k == 0 else move(one, "x", k))

    direction = lax.dot_general(
        in_three(probes), weight, (((1,), (0,)), ((), ())), preferred_element_type=f32
    ).sum(0)
    along = lax.dot_general(
        in_three(direction), around, (((1,), (1,)), ((), ())), preferred_element_type=f32
    ).sum(0)
    along = jnp.roll(along.reshape(4, rows), y, axis=0).reshape(many)
    inner = jnp.sum(
        features.astype(f32).reshape(members, tokens, width) * member_right.astype(f32)[:, None, :],
        axis=2,
    ).reshape(rows)
    left_dot = jnp.sum(left_cols * probe[None, :], axis=1)
    sums = jnp.concatenate([along, placed(inner, y, 4), placed(left_dot, y, 4)])
    sums, parts[1] = lax.optimization_barrier((sums, parts[1]))
    sums = lax.psum(lax.psum(lax.psum(sums, "y"), "x"), "zl")
    along, inner, left_dot = jnp.split(sums, [many, 2 * many])
    inner = spread * inner
    dots = along + inner * jnp.repeat(left_dot, tokens)
    scale = 0.5 / jnp.sqrt(f32(D))
    score = jnp.mean(jnp.tanh(scale * dots).reshape(4, members, tokens), axis=2)
    score = jnp.stack([jnp.where(first, score, 0.0), jnp.where(first, 0.0, score)], axis=1)

    total = sum(p[:cols].astype(f32) for p in parts).astype(bf16)
    lefts = jnp.stack([parts[k][cols:] for k in (0, 3, 2, 1)])
    lefts, total = lax.optimization_barrier((lefts, total))
    lefts = joined(jnp.roll(lefts, x, axis=0).reshape(-1, many), "zl", zl)

    total = total.T.reshape(4, rows, cols)
    parts = []
    for k in range(4):
        one = lax.dynamic_index_in_dim(total, lax.rem(zl + k + 4 - y, 4), 0, keepdims=False)
        parts.append(one if k == 0 else move(one, "zl", k))
    score, parts[1] = lax.optimization_barrier((score, parts[1]))
    score = lax.psum(score.reshape(-1), "c")
    score = lax.psum(placed(score, zh, 4), "zh")
    total = sum(p.astype(f32) for p in parts).astype(bf16)

    total = lax.ppermute(total, ("y", "zl"), turned()).astype(f32)
    inner = lax.dynamic_slice(inner, (y * rows,), (rows,))
    lowrank = inner.reshape(members, tokens)[:, :, None] * left_cols[:, None, :]
    mixed = (total + lowrank.reshape(rows, cols)).astype(bf16)

    labels = jnp.arange(population, dtype=jnp.int32)
    rival = jnp.sum(jnp.where(opponent[:, None] == labels[None, :], score[None, :], 0.0), axis=1)
    fitness = payoff * (score - rival)
    fitness = fitness.reshape(4, 4, 2, members).transpose(1, 2, 0, 3)
    scaled = lefts.reshape(4, 4, 2, members, 192)[..., :block].transpose(0, 2, 1, 3, 4).astype(f32)
    scaled = (fitness[..., None] * scaled).astype(bf16).reshape(population, block)
    term = lax.dot_general(
        scaled, rights.reshape(population, width), (((0,), (0,)), ((), ())),
        preferred_element_type=f32,
    )
    return mixed, term / jnp.sqrt(f32(population))


def solution(mesh):
    fine = Mesh(mesh.devices.reshape(SIZES), AXES)
    member, tensor = ("zh", "y", "c"), ("x", "zl")
    in_specs = (
        P(member, tensor), P(member, tensor), P(member, None), P(member, tensor), P(tensor), P(), P(),
    )
    out_specs = (P(member, tensor), P(member, tensor))
    return jax.shard_map(
        per_device, mesh=fine, in_specs=in_specs, out_specs=out_specs, check_vma=False
    )
```

```python
import jax
import jax.numpy as jnp
from jax import lax
from jax.sharding import Mesh, PartitionSpec as P

D = 5120
FF = 16384
AXES = ("zh", "y", "c", "x", "zl")
SIZES = (4, 4, 2, 4, 4)


def place(*index):
    at = 0
    for i, size in zip(index, SIZES):
        at = at * size + i
    return at


def ring(step):
    return [(i, (i + step) % 4) for i in range(4)]


def swapped():
    return [
        (place(zh, y, c, x, zl), place(x, zl, c, zh, y))
        for zh in range(4) for y in range(4) for c in range(2) for x in range(4) for zl in range(4)
    ]


def turned():
    return [(y * 4 + zl, zl * 4 + y) for y in range(4) for zl in range(4)]


def move(value, axis, step):
    return lax.ppermute(value, axis, ring(step))


def pairs(step):
    return [(i, i ^ step) for i in range(4)]


def joined(value, axis, index):
    for step, later in ((1, index % 2 == 1), (3, index >= 2)):
        got = lax.ppermute(value, axis, pairs(step))
        value = jnp.concatenate([jnp.where(later, got, value), jnp.where(later, value, got)], axis=0)
    return value


def in_three(value):
    terms = []
    for _ in range(3):
        term = lax.reduce_precision(value, 8, 7)
        terms.append(term.astype(jnp.bfloat16))
        value = value - term
    return jnp.stack(terms)


def placed(value, index, count):
    size = value.shape[0]
    return lax.dynamic_update_slice(jnp.zeros((size * count,), value.dtype), value, (index * size,))


def per_device(features, down_weight, member_left, member_right, probe, payoff, opponent):
    f32, bf16 = jnp.float32, jnp.bfloat16
    rows, width = features.shape
    members = member_right.shape[0]
    tokens = rows // members
    population = payoff.shape[0]
    block = down_weight.shape[0]
    cols = probe.shape[0]
    spread = 1.0 / jnp.sqrt(f32(FF))
    zh, y, c, x, zl = (lax.axis_index(a) for a in AXES)
    first = c == 0
    many = 4 * rows

    own = jnp.concatenate([down_weight, member_right], axis=0)
    stack = lax.all_gather(own, ("zh", "c"), axis=0, tiled=True).reshape(4, 2, -1, width)
    weight = stack[:, :, :block].reshape(-1, width)
    rights = lax.all_gather(stack[:, :, block:], "y", axis=0, tiled=False)

    around = [features] + [move(features, "y", -j) for j in (1, 2, 3)]

    probes = lax.psum(placed(probe, x, 4), "x")
    probes = lax.ppermute(probes, ("y", "zl"), turned())

    left_cols = lax.dynamic_slice(member_left, (0, (x * 4 + zl) * cols), (members, cols))
    lefts = lax.ppermute(left_cols, AXES, swapped())
    mine = jnp.where(first, lefts[:, :block], lefts[:, block:])
    other = jnp.where(first, lefts[:, block:], lefts[:, :block])
    other = lax.ppermute(other, "c", [(0, 1), (1, 0)])
    lefts = jnp.where(first, jnp.concatenate([mine, other], 0), jnp.concatenate([other, mine], 0))
    lefts = jnp.pad(lefts, ((0, 0), (0, 192 - block))).reshape(-1, many)
    lefts = joined(lefts, "x", x)
    left_cols = left_cols.astype(f32)

    part = lax.dot_general(
        weight, jnp.concatenate(around, axis=0), (((1,), (1,)), ((), ())), preferred_element_type=f32
    ).astype(bf16).reshape(4, cols, many)
    parts = []
    for k in range(4):
        one = lax.dynamic_index_in_dim(part, lax.rem(x + k, 4), 0, keepdims=False)
        parts.append(one if k == 0 else move(one, "x", k))

    direction = lax.dot_general(
        in_three(probes), weight, (((1,), (0,)), ((), ())), preferred_element_type=f32
    ).sum(0)
    along = jnp.stack([
        lax.dot_general(
            in_three(direction), f, (((1,), (1,)), ((), ())), preferred_element_type=f32
        ).sum(0)
        for f in around
    ])
    along = jnp.roll(along, y, axis=0).reshape(many)
    inner = jnp.sum(
        features.astype(f32).reshape(members, tokens, width) * member_right.astype(f32)[:, None, :],
        axis=2,
    ).reshape(rows)
    left_dot = jnp.sum(left_cols * probe[None, :], axis=1)
    sums = jnp.concatenate([along, placed(inner, y, 4), placed(left_dot, y, 4)])
    sums, lefts, parts[1] = lax.optimization_barrier((sums, lefts, parts[1]))
    sums = lax.psum(lax.psum(sums, "y"), "x")
    lefts = joined(lefts, "zl", zl)
    total = sum(p.astype(f32) for p in parts).astype(bf16)
    sums, lefts, total = lax.optimization_barrier((sums, lefts, total))

    sums = lax.psum(sums, "zl")
    total = total.T.reshape(4, rows, cols)
    parts = []
    for k in range(4):
        one = lax.dynamic_index_in_dim(total, lax.rem(zl + k + 4 - y, 4), 0, keepdims=False)
        parts.append(one if k == 0 else move(one, "zl", k))
    total = sum(p.astype(f32) for p in parts).astype(bf16)
    sums, total = lax.optimization_barrier((sums, total))
    along, inner, left_dot = jnp.split(sums, [many, 2 * many])
    inner = spread * inner
    dots = along + inner * jnp.repeat(left_dot, tokens)
    scale = 0.5 / jnp.sqrt(f32(D))
    score = jnp.mean(jnp.tanh(scale * dots).reshape(4, members, tokens), axis=2)
    score = jnp.stack([jnp.where(first, score, 0.0), jnp.where(first, 0.0, score)], axis=1)

    score = lax.psum(score.reshape(-1), "c")
    score = lax.psum(placed(score, zh, 4), "zh")

    total = lax.ppermute(total, ("y", "zl"), turned()).astype(f32)
    inner = lax.dynamic_slice(inner, (y * rows,), (rows,))
    lowrank = inner.reshape(members, tokens)[:, :, None] * left_cols[:, None, :]
    mixed = (total + lowrank.reshape(rows, cols)).astype(bf16)

    labels = jnp.arange(population, dtype=jnp.int32)
    rival = jnp.sum(jnp.where(opponent[:, None] == labels[None, :], score[None, :], 0.0), axis=1)
    fitness = payoff * (score - rival)
    fitness = fitness.reshape(4, 4, -1).transpose(1, 0, 2).reshape(population, 1)
    scaled = lefts.reshape(population, 192)[:, :block].astype(f32)
    scaled = (fitness * scaled).astype(bf16)
    term = lax.dot_general(
        scaled, rights.reshape(population, width), (((0,), (0,)), ((), ())),
        preferred_element_type=f32,
    )
    return mixed, term / jnp.sqrt(f32(population))


def solution(mesh):
    fine = Mesh(mesh.devices.reshape(SIZES), AXES)
    member, tensor = ("zh", "y", "c"), ("x", "zl")
    in_specs = (
        P(member, tensor), P(member, tensor), P(member, None), P(member, tensor), P(tensor), P(), P(),
    )
    out_specs = (P(member, tensor), P(member, tensor))
    return jax.shard_map(
        per_device, mesh=fine, in_specs=in_specs, out_specs=out_specs, check_vma=False
    )
```

```python
import jax
import jax.numpy as jnp
from jax import lax
from jax.sharding import Mesh, PartitionSpec as P

D = 5120
FF = 16384
AXES = ("zh", "y", "c", "x", "zl")
SIZES = (4, 4, 2, 4, 4)


def place(*index):
    at = 0
    for i, size in zip(index, SIZES):
        at = at * size + i
    return at


def ring(step):
    return [(i, (i + step) % 4) for i in range(4)]


def swapped(flip):
    return [
        (place(zh, y, c, x, zl), place(x, zl, c ^ flip, zh, y))
        for zh in range(4) for y in range(4) for c in range(2) for x in range(4) for zl in range(4)
    ]


def turned():
    return [(y * 4 + zl, zl * 4 + y) for y in range(4) for zl in range(4)]


def move(value, axis, step):
    return lax.ppermute(value, axis, ring(step))


def pairs(step):
    return [(i, i ^ step) for i in range(4)]


def joined(value, axis, index):
    for step, later in ((1, index % 2 == 1), (3, index >= 2)):
        got = lax.ppermute(value, axis, pairs(step))
        value = jnp.concatenate([jnp.where(later, got, value), jnp.where(later, value, got)], axis=0)
    return value


def in_three(value):
    terms = []
    for _ in range(3):
        term = lax.reduce_precision(value, 8, 7)
        terms.append(term.astype(jnp.bfloat16))
        value = value - term
    return jnp.stack(terms)


def pack(value, width):
    terms = in_three(value).reshape(-1)
    return jnp.pad(terms, (0, -terms.shape[0] % (8 * width))).reshape(-1, width)


def unpack(rows, size):
    return rows.reshape(-1)[: 3 * size].reshape(3, size).sum(0)


def placed(value, index, count):
    size = value.shape[0]
    return lax.dynamic_update_slice(jnp.zeros((size * count,), value.dtype), value, (index * size,))


def per_device(features, down_weight, member_left, member_right, probe, payoff, opponent):
    f32, bf16 = jnp.float32, jnp.bfloat16
    rows, width = features.shape
    members = member_right.shape[0]
    tokens = rows // members
    population = payoff.shape[0]
    block = down_weight.shape[0]
    cols = probe.shape[0]
    spread = 1.0 / jnp.sqrt(f32(FF))
    zh, y, c, x, zl = (lax.axis_index(a) for a in AXES)
    first = c == 0
    many = 4 * rows

    own = jnp.concatenate([down_weight, member_right], axis=0)
    stack = lax.all_gather(own, ("zh", "c"), axis=0, tiled=True).reshape(4, 2, -1, width)
    weight = stack[:, :, :block].reshape(-1, width)
    rights = lax.all_gather(stack[:, :, block:], "y", axis=0, tiled=False)

    left_cols = lax.dynamic_slice(member_left, (0, (x * 4 + zl) * cols), (members, cols)).astype(f32)
    payload = jnp.concatenate([left_cols, probe[None, :]], axis=0)
    mine = jnp.where(first, payload[:, :block], payload[:, block:])
    other = jnp.where(first, left_cols[:, block:], left_cols[:, :block])
    mine = lax.ppermute(mine, AXES, swapped(0))
    other = lax.ppermute(other, AXES, swapped(1))
    mine, other = lax.optimization_barrier((mine, other))

    direction = jnp.sum(down_weight.astype(f32) * mine[members][:, None], axis=0)
    inner = jnp.sum(
        features.astype(f32).reshape(members, tokens, width) * member_right.astype(f32)[:, None, :],
        axis=2,
    ).reshape(rows)
    left_dot = jnp.sum(left_cols * probe[None, :], axis=1)
    here = y * 2 + c
    early = jnp.concatenate([direction, placed(inner, here, 8), placed(left_dot, here, 8)])
    early = lax.psum(early, ("y", "c"))

    features, early = lax.optimization_barrier((features, early))
    around = [features] + [move(features, "y", -j) for j in (1, 2, 3)]
    direction, inner, left_dot = jnp.split(early, [width, width + 2 * many])
    direction = lax.psum(direction, "zh")

    mine = mine[:members]
    lefts = jnp.where(first, jnp.concatenate([mine, other], 0), jnp.concatenate([other, mine], 0))
    lefts = jnp.pad(lefts.astype(bf16), ((0, 0), (0, 192 - block))).reshape(-1, many)
    lefts = joined(lefts, "x", x)

    along = jnp.stack([
        lax.dot_general(
            in_three(direction), f, (((1,), (1,)), ((), ())), preferred_element_type=f32
        ).sum(0)
        for f in around
    ])
    along = jnp.roll(along, y, axis=0).reshape(many)
    inner, left_dot = inner.reshape(4, 2, -1), left_dot.reshape(4, 2, -1)
    inner = jnp.where(first, inner[:, 0], inner[:, 1]).reshape(-1)
    left_dot = jnp.where(first, left_dot[:, 0], left_dot[:, 1]).reshape(-1)
    sums = jnp.concatenate([along, inner, left_dot])
    size = sums.shape[0]

    part = lax.dot_general(
        weight, jnp.concatenate(around, axis=0), (((1,), (1,)), ((), ())), preferred_element_type=f32
    ).astype(bf16).reshape(4, cols, many)
    ride = pack(sums, many)
    parts = []
    for k in range(4):
        one = lax.dynamic_index_in_dim(part, lax.rem(x + k, 4), 0, keepdims=False)
        one = jnp.concatenate([one, ride], axis=0)
        parts.append(one if k == 0 else move(one, "x", k))
    lefts, parts[1] = lax.optimization_barrier((lefts, parts[1]))
    lefts = joined(lefts, "zl", zl)
    total = sum(p.astype(f32) for p in parts)
    ride = pack(unpack(total[cols:], size), cols)

    total = total[:cols].astype(bf16).T.reshape(4, rows, cols)
    parts = []
    for k in range(4):
        one = lax.dynamic_index_in_dim(total, lax.rem(zl + k + 4 - y, 4), 0, keepdims=False)
        one = jnp.concatenate([one, ride], axis=0)
        parts.append(one if k == 0 else move(one, "zl", k))
    total = sum(p.astype(f32) for p in parts)
    sums = unpack(total[rows:], size)
    total = total[:rows].astype(bf16)


    along, inner, left_dot = jnp.split(sums, [many, 2 * many])
    inner = spread * inner
    dots = along + inner * jnp.repeat(left_dot, tokens)
    scale = 0.5 / jnp.sqrt(f32(D))
    score = jnp.mean(jnp.tanh(scale * dots).reshape(4, members, tokens), axis=2)
    score = jnp.stack([jnp.where(first, score, 0.0), jnp.where(first, 0.0, score)], axis=1)

    score = lax.psum(score.reshape(-1), "c")
    score = lax.psum(placed(score, zh, 4), "zh")

    total = lax.ppermute(total, ("y", "zl"), turned()).astype(f32)
    inner = lax.dynamic_slice(inner, (y * rows,), (rows,))
    lowrank = inner.reshape(members, tokens)[:, :, None] * left_cols[:, None, :]
    mixed = (total + lowrank.reshape(rows, cols)).astype(bf16)

    labels = jnp.arange(population, dtype=jnp.int32)
    rival = jnp.sum(jnp.where(opponent[:, None] == labels[None, :], score[None, :], 0.0), axis=1)
    fitness = payoff * (score - rival)
    fitness = fitness.reshape(4, 4, -1).transpose(1, 0, 2).reshape(population, 1)
    scaled = lefts.reshape(population, 192)[:, :block].astype(f32)
    scaled = (fitness * scaled).astype(bf16)
    term = lax.dot_general(
        scaled, rights.reshape(population, width), (((0,), (0,)), ((), ())),
        preferred_element_type=f32,
    )
    return mixed, term / jnp.sqrt(f32(population))


def solution(mesh):
    fine = Mesh(mesh.devices.reshape(SIZES), AXES)
    member, tensor = ("zh", "y", "c"), ("x", "zl")
    in_specs = (
        P(member, tensor), P(member, tensor), P(member, None), P(member, tensor), P(tensor), P(), P(),
    )
    out_specs = (P(member, tensor), P(member, tensor))
    return jax.shard_map(
        per_device, mesh=fine, in_specs=in_specs, out_specs=out_specs, check_vma=False
    )
```

```python
import jax
import jax.numpy as jnp
from jax import lax
from jax.sharding import Mesh, PartitionSpec as P

D = 5120
FF = 16384
AXES = ("zh", "y", "c", "x", "zl")
SIZES = (4, 4, 2, 4, 4)


def place(*index):
    at = 0
    for i, size in zip(index, SIZES):
        at = at * size + i
    return at


def ring(step):
    return [(i, (i + step) % 4) for i in range(4)]


def swapped(flip):
    return [
        (place(zh, y, c, x, zl), place(x, zl, c ^ flip, zh, y))
        for zh in range(4) for y in range(4) for c in range(2) for x in range(4) for zl in range(4)
    ]


def turned():
    return [(y * 4 + zl, zl * 4 + y) for y in range(4) for zl in range(4)]


def move(value, axis, step):
    return lax.ppermute(value, axis, ring(step))


def pairs(step):
    return [(i, i ^ step) for i in range(4)]


def joined(value, axis, index):
    for step, later in ((1, index % 2 == 1), (3, index >= 2)):
        got = lax.ppermute(value, axis, pairs(step))
        value = jnp.concatenate([jnp.where(later, got, value), jnp.where(later, value, got)], axis=0)
    return value


def in_three(value):
    terms = []
    for _ in range(3):
        term = lax.reduce_precision(value, 8, 7)
        terms.append(term.astype(jnp.bfloat16))
        value = value - term
    return jnp.stack(terms)


def pack(value, width):
    terms = in_three(value).reshape(-1)
    return jnp.pad(terms, (0, -terms.shape[0] % (8 * width))).reshape(-1, width)


def unpack(rows, size):
    return rows.reshape(-1)[: 3 * size].reshape(3, size).sum(0)


def placed(value, index, count):
    size = value.shape[0]
    return lax.dynamic_update_slice(jnp.zeros((size * count,), value.dtype), value, (index * size,))


def per_device(features, down_weight, member_left, member_right, probe, payoff, opponent):
    f32, bf16 = jnp.float32, jnp.bfloat16
    rows, width = features.shape
    members = member_right.shape[0]
    tokens = rows // members
    population = payoff.shape[0]
    block = down_weight.shape[0]
    cols = probe.shape[0]
    spread = 1.0 / jnp.sqrt(f32(FF))
    zh, y, c, x, zl = (lax.axis_index(a) for a in AXES)
    first = c == 0
    many = 4 * rows

    own = jnp.concatenate([down_weight, member_right], axis=0)
    stack = lax.all_gather(own, ("zh", "c"), axis=0, tiled=True).reshape(4, 2, -1, width)
    weight = stack[:, :, :block].reshape(-1, width)
    rights = lax.all_gather(stack[:, :, block:], "y", axis=0, tiled=False)

    left_cols = lax.dynamic_slice(member_left, (0, (x * 4 + zl) * cols), (members, cols)).astype(f32)
    payload = jnp.concatenate([left_cols, probe[None, :]], axis=0)
    mine = jnp.where(first, payload[:, :block], payload[:, block:])
    other = jnp.where(first, left_cols[:, block:], left_cols[:, :block])
    mine = lax.ppermute(mine, AXES, swapped(0))
    other = lax.ppermute(other, AXES, swapped(1))
    mine, other = lax.optimization_barrier((mine, other))

    direction = jnp.sum(down_weight.astype(f32) * mine[members][:, None], axis=0)
    inner = jnp.sum(
        features.astype(f32).reshape(members, tokens, width) * member_right.astype(f32)[:, None, :],
        axis=2,
    ).reshape(rows)
    left_dot = jnp.sum(left_cols * probe[None, :], axis=1)
    direction = lax.psum(direction, "c")
    early = jnp.concatenate([direction, placed(inner, y, 4), placed(left_dot, y, 4)])
    early = lax.psum(early, "y")

    features, early = lax.optimization_barrier((features, early))
    around = [features] + [move(features, "y", -j) for j in (1, 2, 3)]
    direction, inner, left_dot = jnp.split(early, [width, width + many])
    direction = lax.psum(direction, "zh")

    mine = mine[:members]
    lefts = jnp.where(first, jnp.concatenate([mine, other], 0), jnp.concatenate([other, mine], 0))
    lefts = jnp.pad(lefts.astype(bf16), ((0, 0), (0, 192 - block))).reshape(-1, many)

    along = jnp.stack([
        lax.dot_general(
            in_three(direction), f, (((1,), (1,)), ((), ())), preferred_element_type=f32
        ).sum(0)
        for f in around
    ])
    along = jnp.roll(along, y, axis=0).reshape(many)
    sums = jnp.concatenate([along, inner, left_dot])
    size = sums.shape[0]

    part = lax.dot_general(
        weight, jnp.concatenate(around, axis=0), (((1,), (1,)), ((), ())), preferred_element_type=f32
    ).astype(bf16).reshape(4, cols, many)
    ride = jnp.concatenate([pack(sums, many), lefts], axis=0)
    end = part.shape[1] + ride.shape[0] - lefts.shape[0]
    parts = []
    for k in range(4):
        one = lax.dynamic_index_in_dim(part, lax.rem(x + k, 4), 0, keepdims=False)
        one = jnp.concatenate([one, ride], axis=0)
        parts.append(one if k == 0 else move(one, "x", k))
    total = sum(p[:end].astype(f32) for p in parts)
    lefts = jnp.stack([parts[k][end:] for k in (0, 3, 2, 1)])
    lefts, total = lax.optimization_barrier((lefts, total))
    lefts = joined(jnp.roll(lefts, x, axis=0).reshape(-1, many), "zl", zl)
    ride = pack(unpack(total[cols:], size), cols)

    total = total[:cols].astype(bf16).T.reshape(4, rows, cols)
    parts = []
    for k in range(4):
        one = lax.dynamic_index_in_dim(total, lax.rem(zl + k + 4 - y, 4), 0, keepdims=False)
        one = jnp.concatenate([one, ride], axis=0)
        parts.append(one if k == 0 else move(one, "zl", k))
    total = sum(p.astype(f32) for p in parts)
    sums = unpack(total[rows:], size)
    total = total[:rows].astype(bf16)

    along, inner, left_dot = jnp.split(sums, [many, 2 * many])
    inner = spread * inner
    dots = along + inner * jnp.repeat(left_dot, tokens)
    scale = 0.5 / jnp.sqrt(f32(D))
    score = jnp.mean(jnp.tanh(scale * dots).reshape(4, members, tokens), axis=2)
    score = jnp.stack([jnp.where(first, score, 0.0), jnp.where(first, 0.0, score)], axis=1)
    score = lax.psum(score.reshape(-1), "c")
    score = lax.psum(placed(score, zh, 4), "zh")

    total = lax.ppermute(total, ("y", "zl"), turned()).astype(f32)
    inner = lax.dynamic_slice(inner, (y * rows,), (rows,))
    lowrank = inner.reshape(members, tokens)[:, :, None] * left_cols[:, None, :]
    mixed = (total + lowrank.reshape(rows, cols)).astype(bf16)

    labels = jnp.arange(population, dtype=jnp.int32)
    rival = jnp.sum(jnp.where(opponent[:, None] == labels[None, :], score[None, :], 0.0), axis=1)
    fitness = payoff * (score - rival)
    fitness = fitness.reshape(4, 4, -1).transpose(1, 0, 2).reshape(population, 1)
    scaled = lefts.reshape(population, 192)[:, :block].astype(f32)
    scaled = (fitness * scaled).astype(bf16)
    term = lax.dot_general(
        scaled, rights.reshape(population, width), (((0,), (0,)), ((), ())),
        preferred_element_type=f32,
    )
    return mixed, term / jnp.sqrt(f32(population))


def solution(mesh):
    fine = Mesh(mesh.devices.reshape(SIZES), AXES)
    member, tensor = ("zh", "y", "c"), ("x", "zl")
    in_specs = (
        P(member, tensor), P(member, tensor), P(member, None), P(member, tensor), P(tensor), P(), P(),
    )
    out_specs = (P(member, tensor), P(member, tensor))
    return jax.shard_map(
        per_device, mesh=fine, in_specs=in_specs, out_specs=out_specs, check_vma=False
    )
```

```python
import jax
import jax.numpy as jnp
from jax import lax
from jax.sharding import Mesh, PartitionSpec as P

D = 5120
FF = 16384
AXES = ("zh", "y", "c", "x", "zl")
SIZES = (4, 4, 2, 4, 4)


def place(*index):
    at = 0
    for i, size in zip(index, SIZES):
        at = at * size + i
    return at


def ring(step):
    return [(i, (i + step) % 4) for i in range(4)]


def swapped():
    return [
        (place(zh, y, c, x, zl), place(x, zl, c, zh, y))
        for zh in range(4) for y in range(4) for c in range(2) for x in range(4) for zl in range(4)
    ]


def turned():
    return [(y * 4 + zl, zl * 4 + y) for y in range(4) for zl in range(4)]


def move(value, axis, step):
    return lax.ppermute(value, axis, ring(step))


def pairs(step):
    return [(i, i ^ step) for i in range(4)]


def joined(value, axis, index):
    for step, later in ((1, index % 2 == 1), (3, index >= 2)):
        got = lax.ppermute(value, axis, pairs(step))
        value = jnp.concatenate([jnp.where(later, got, value), jnp.where(later, value, got)], axis=0)
    return value


def in_three(value):
    terms = []
    for _ in range(3):
        term = lax.reduce_precision(value, 8, 7)
        terms.append(term.astype(jnp.bfloat16))
        value = value - term
    return jnp.stack(terms)


def pack(value, width):
    terms = in_three(value).reshape(-1)
    return jnp.pad(terms, (0, -terms.shape[0] % (8 * width))).reshape(-1, width)


def unpack(rows, size):
    return rows.reshape(-1)[: 3 * size].reshape(3, size).sum(0)


def placed(value, index, count):
    size = value.shape[0]
    return lax.dynamic_update_slice(jnp.zeros((size * count,), value.dtype), value, (index * size,))


def per_device(features, down_weight, member_left, member_right, probe, payoff, opponent):
    f32, bf16 = jnp.float32, jnp.bfloat16
    rows, width = features.shape
    members = member_right.shape[0]
    tokens = rows // members
    population = payoff.shape[0]
    block = down_weight.shape[0]
    cols = probe.shape[0]
    spread = 1.0 / jnp.sqrt(f32(FF))
    zh, y, c, x, zl = (lax.axis_index(a) for a in AXES)
    first = c == 0
    many = 4 * rows

    lead = 128
    rest = block - lead
    weight_one = lax.all_gather(down_weight[:lead], ("zh", "c"), axis=0, tiled=True)

    around = [features] + [move(features, "y", -j) for j in (1, 2, 3)]

    probes = lax.psum(placed(probe, x, 4), "x")
    probes = lax.ppermute(probes, ("y", "zl"), turned())

    left_cols = lax.dynamic_slice(member_left, (0, (x * 4 + zl) * cols), (members, cols))
    lefts = lax.ppermute(left_cols, AXES, swapped())
    own = jnp.concatenate([down_weight[lead:], member_right], axis=0)
    own, lefts = lax.optimization_barrier((own, lefts))
    stack = lax.all_gather(own, ("zh", "c"), axis=0, tiled=True).reshape(4, 2, -1, width)
    mine = jnp.where(first, lefts[:, :block], lefts[:, block:])
    other = jnp.where(first, lefts[:, block:], lefts[:, :block])
    other = lax.ppermute(other, "c", [(0, 1), (1, 0)])
    lefts = jnp.where(first, jnp.concatenate([mine, other], 0), jnp.concatenate([other, mine], 0))
    lefts = jnp.pad(lefts, ((0, 0), (0, 192 - block))).reshape(-1, many)
    lefts = joined(lefts, "x", x)
    left_cols = left_cols.astype(f32)

    def products(weight):
        part = lax.dot_general(
            weight, jnp.concatenate(around, axis=0), (((1,), (1,)), ((), ())),
            preferred_element_type=f32,
        ).astype(bf16).reshape(4, -1, many)
        return [
            lax.dynamic_index_in_dim(part, lax.rem(x + k, 4), 0, keepdims=False) for k in range(4)
        ]

    ones = products(weight_one)
    ones = [ones[0]] + [move(ones[k], "x", k) for k in (1, 2, 3)]
    lefts, stack, ones = lax.optimization_barrier((lefts, stack, ones))
    weight_two = stack[:, :, :rest].reshape(-1, width)
    rights = lax.all_gather(stack[:, :, rest:], "y", axis=0, tiled=False)
    lefts = joined(lefts, "zl", zl)

    probes = probes.reshape(4, 2, block)
    direction = sum(
        lax.dot_general(
            in_three(p.reshape(-1)), w, (((1,), (0,)), ((), ())), preferred_element_type=f32
        ).sum(0)
        for p, w in ((probes[:, :, :lead], weight_one), (probes[:, :, lead:], weight_two))
    )
    along = jnp.stack([
        lax.dot_general(
            in_three(direction), f, (((1,), (1,)), ((), ())), preferred_element_type=f32
        ).sum(0)
        for f in around
    ])
    along = jnp.roll(along, y, axis=0).reshape(many)
    inner = jnp.sum(
        features.astype(f32).reshape(members, tokens, width) * member_right.astype(f32)[:, None, :],
        axis=2,
    ).reshape(rows)
    left_dot = jnp.sum(left_cols * probe[None, :], axis=1)
    sums = jnp.concatenate([along, placed(inner, y, 4), placed(left_dot, y, 4)])
    size = sums.shape[0]
    ride = pack(sums, many)
    twos = [jnp.concatenate([p, ride], axis=0) for p in products(weight_two)]
    twos = [twos[0]] + [move(twos[k], "x", k) for k in (1, 2, 3)]
    total_one = sum(p.astype(f32) for p in ones).astype(bf16)
    total_two = sum(p.astype(f32) for p in twos)
    ride = pack(unpack(total_two[2 * rest :], size), cols)
    total_two = total_two[: 2 * rest].astype(bf16)
    total = jnp.concatenate(
        [total_one.reshape(2, lead, many), total_two.reshape(2, rest, many)], axis=1
    ).reshape(cols, many)

    total = total.T.reshape(4, rows, cols)
    parts = []
    for k in range(4):
        one = lax.dynamic_index_in_dim(total, lax.rem(zl + k + 4 - y, 4), 0, keepdims=False)
        one = jnp.concatenate([one, ride], axis=0)
        parts.append(one if k == 0 else move(one, "zl", k))
    total = sum(p.astype(f32) for p in parts)
    sums = lax.psum(unpack(total[rows:], size), "y")
    total = total[:rows].astype(bf16)

    along, inner, left_dot = jnp.split(sums, [many, 2 * many])
    inner = spread * inner
    dots = along + inner * jnp.repeat(left_dot, tokens)
    scale = 0.5 / jnp.sqrt(f32(D))
    score = jnp.mean(jnp.tanh(scale * dots).reshape(4, members, tokens), axis=2)
    score = jnp.stack([jnp.where(first, score, 0.0), jnp.where(first, 0.0, score)], axis=1)

    score = lax.psum(score.reshape(-1), "c")
    score = lax.psum(placed(score, zh, 4), "zh")

    total = lax.ppermute(total, ("y", "zl"), turned()).astype(f32)
    inner = lax.dynamic_slice(inner, (y * rows,), (rows,))
    lowrank = inner.reshape(members, tokens)[:, :, None] * left_cols[:, None, :]
    mixed = (total + lowrank.reshape(rows, cols)).astype(bf16)

    labels = jnp.arange(population, dtype=jnp.int32)
    rival = jnp.sum(jnp.where(opponent[:, None] == labels[None, :], score[None, :], 0.0), axis=1)
    fitness = payoff * (score - rival)
    fitness = fitness.reshape(4, 4, -1).transpose(1, 0, 2).reshape(population, 1)
    scaled = lefts.reshape(population, 192)[:, :block].astype(f32)
    scaled = (fitness * scaled).astype(bf16)
    term = lax.dot_general(
        scaled, rights.reshape(population, width), (((0,), (0,)), ((), ())),
        preferred_element_type=f32,
    )
    return mixed, term / jnp.sqrt(f32(population))


def solution(mesh):
    fine = Mesh(mesh.devices.reshape(SIZES), AXES)
    member, tensor = ("zh", "y", "c"), ("x", "zl")
    in_specs = (
        P(member, tensor), P(member, tensor), P(member, None), P(member, tensor), P(tensor), P(), P(),
    )
    out_specs = (P(member, tensor), P(member, tensor))
    return jax.shard_map(
        per_device, mesh=fine, in_specs=in_specs, out_specs=out_specs, check_vma=False
    )
```

```python
import jax
import jax.numpy as jnp
from jax import lax
from jax.sharding import Mesh, PartitionSpec as P

D = 5120
FF = 16384
AXES = ("zh", "y", "c", "x", "zl")
SIZES = (4, 4, 2, 4, 4)


def place(*index):
    at = 0
    for i, size in zip(index, SIZES):
        at = at * size + i
    return at


def ring(step):
    return [(i, (i + step) % 4) for i in range(4)]


def swapped(flip):
    return [
        (place(zh, y, c, x, zl), place(x, zl, c ^ flip, zh, y))
        for zh in range(4) for y in range(4) for c in range(2) for x in range(4) for zl in range(4)
    ]


def turned():
    return [(y * 4 + zl, zl * 4 + y) for y in range(4) for zl in range(4)]


def move(value, axis, step):
    return lax.ppermute(value, axis, ring(step))


def pairs(step):
    return [(i, i ^ step) for i in range(4)]


def joined(value, axis, index):
    for step, later in ((1, index % 2 == 1), (3, index >= 2)):
        got = lax.ppermute(value, axis, pairs(step))
        value = jnp.concatenate([jnp.where(later, got, value), jnp.where(later, value, got)], axis=0)
    return value


def in_three(value):
    terms = []
    for _ in range(3):
        term = lax.reduce_precision(value, 8, 7)
        terms.append(term.astype(jnp.bfloat16))
        value = value - term
    return jnp.stack(terms)


def pack(value, width):
    terms = in_three(value).reshape(-1)
    return jnp.pad(terms, (0, -terms.shape[0] % (8 * width))).reshape(-1, width)


def unpack(rows, size):
    return rows.reshape(-1)[: 3 * size].reshape(3, size).sum(0)


def placed(value, index, count):
    size = value.shape[0]
    return lax.dynamic_update_slice(jnp.zeros((size * count,), value.dtype), value, (index * size,))


def per_device(features, down_weight, member_left, member_right, probe, payoff, opponent):
    f32, bf16 = jnp.float32, jnp.bfloat16
    rows, width = features.shape
    members = member_right.shape[0]
    tokens = rows // members
    population = payoff.shape[0]
    block = down_weight.shape[0]
    cols = probe.shape[0]
    spread = 1.0 / jnp.sqrt(f32(FF))
    zh, y, c, x, zl = (lax.axis_index(a) for a in AXES)
    first = c == 0
    many = 4 * rows

    own = jnp.concatenate([down_weight, member_right], axis=0)
    stack = lax.all_gather(own, ("zh", "c"), axis=0, tiled=True).reshape(4, 2, -1, width)
    weight = stack[:, :, :block].reshape(-1, width)
    rights = lax.all_gather(stack[:, :, block:], "y", axis=0, tiled=False)

    left_cols = lax.dynamic_slice(member_left, (0, (x * 4 + zl) * cols), (members, cols)).astype(f32)
    payload = jnp.concatenate([left_cols, probe[None, :]], axis=0)
    mine = jnp.where(first, payload[:, :block], payload[:, block:])
    other = jnp.where(first, left_cols[:, block:], left_cols[:, :block])
    mine = lax.ppermute(mine, AXES, swapped(0))
    other = lax.ppermute(other, AXES, swapped(1))
    mine, other = lax.optimization_barrier((mine, other))

    direction = jnp.sum(down_weight.astype(f32) * mine[members][:, None], axis=0)
    inner = jnp.sum(
        features.astype(f32).reshape(members, tokens, width) * member_right.astype(f32)[:, None, :],
        axis=2,
    ).reshape(rows)
    left_dot = jnp.sum(left_cols * probe[None, :], axis=1)
    direction = lax.psum(direction, "c")
    early = jnp.concatenate([direction, placed(inner, y, 4), placed(left_dot, y, 4)])
    early = lax.psum(early, "y")

    features, early = lax.optimization_barrier((features, early))
    around = [features] + [move(features, "y", -j) for j in (1, 2, 3)]
    direction, inner, left_dot = jnp.split(early, [width, width + many])
    direction = lax.psum(direction, "zh")

    mine = mine[:members]
    lefts = jnp.where(first, jnp.concatenate([mine, other], 0), jnp.concatenate([other, mine], 0))
    lefts = jnp.pad(lefts.astype(bf16), ((0, 0), (0, 192 - block))).reshape(-1, many)

    along = jnp.stack([
        lax.dot_general(
            in_three(direction), f, (((1,), (1,)), ((), ())), preferred_element_type=f32
        ).sum(0)
        for f in around
    ])
    along = jnp.roll(along, y, axis=0).reshape(many)
    sums = jnp.concatenate([along, inner, left_dot])
    size = sums.shape[0]

    part = lax.dot_general(
        weight, jnp.concatenate(around, axis=0), (((1,), (1,)), ((), ())), preferred_element_type=f32
    ).astype(bf16).reshape(4, cols, many)
    ride = jnp.concatenate([pack(sums, many), lefts], axis=0)
    end = part.shape[1] + ride.shape[0] - lefts.shape[0]
    parts = [
        jnp.concatenate([
            lax.dynamic_index_in_dim(part, lax.rem(x + k, 4), 0, keepdims=False), ride
        ], axis=0)
        for k in range(4)
    ]
    cut = 168
    near = parts[3]
    passing = move(parts[2][:cut], "x", -1)
    two = move(parts[2][cut:], "x", 2)
    passing, two = lax.optimization_barrier((passing, two))
    one = move(parts[1], "x", 1)
    added = (near[:cut].astype(f32) + passing.astype(f32)).astype(bf16)
    near = jnp.concatenate([added, near[cut:]], axis=0)
    three = move(near, "x", -1)
    total = parts[0][:end].astype(f32) + one[:end].astype(f32) + three[:end].astype(f32)
    total = jnp.concatenate([total[:cut], total[cut:] + two[: end - cut].astype(f32)], axis=0)
    lefts = jnp.stack([parts[0][end:], three[end:], two[end - cut :], one[end:]])
    lefts, total = lax.optimization_barrier((lefts, total))
    lefts = joined(jnp.roll(lefts, x, axis=0).reshape(-1, many), "zl", zl)
    ride = pack(unpack(total[cols:], size), cols)

    total = total[:cols].astype(bf16).T.reshape(4, rows, cols)
    parts = []
    for k in range(4):
        one = lax.dynamic_index_in_dim(total, lax.rem(zl + k + 4 - y, 4), 0, keepdims=False)
        one = jnp.concatenate([one, ride], axis=0)
        parts.append(one if k == 0 else move(one, "zl", k))
    total = sum(p.astype(f32) for p in parts)
    sums = unpack(total[rows:], size)
    total = total[:rows].astype(bf16)

    along, inner, left_dot = jnp.split(sums, [many, 2 * many])
    inner = spread * inner
    dots = along + inner * jnp.repeat(left_dot, tokens)
    scale = 0.5 / jnp.sqrt(f32(D))
    score = jnp.mean(jnp.tanh(scale * dots).reshape(4, members, tokens), axis=2)
    score = jnp.stack([jnp.where(first, score, 0.0), jnp.where(first, 0.0, score)], axis=1)
    score = lax.psum(score.reshape(-1), "c")
    score = lax.psum(placed(score, zh, 4), "zh")

    total = lax.ppermute(total, ("y", "zl"), turned()).astype(f32)
    inner = lax.dynamic_slice(inner, (y * rows,), (rows,))
    lowrank = inner.reshape(members, tokens)[:, :, None] * left_cols[:, None, :]
    mixed = (total + lowrank.reshape(rows, cols)).astype(bf16)

    labels = jnp.arange(population, dtype=jnp.int32)
    rival = jnp.sum(jnp.where(opponent[:, None] == labels[None, :], score[None, :], 0.0), axis=1)
    fitness = payoff * (score - rival)
    fitness = fitness.reshape(4, 4, -1).transpose(1, 0, 2).reshape(population, 1)
    scaled = lefts.reshape(population, 192)[:, :block].astype(f32)
    scaled = (fitness * scaled).astype(bf16)
    term = lax.dot_general(
        scaled, rights.reshape(population, width), (((0,), (0,)), ((), ())),
        preferred_element_type=f32,
    )
    return mixed, term / jnp.sqrt(f32(population))


def solution(mesh):
    fine = Mesh(mesh.devices.reshape(SIZES), AXES)
    member, tensor = ("zh", "y", "c"), ("x", "zl")
    in_specs = (
        P(member, tensor), P(member, tensor), P(member, None), P(member, tensor), P(tensor), P(), P(),
    )
    out_specs = (P(member, tensor), P(member, tensor))
    return jax.shard_map(
        per_device, mesh=fine, in_specs=in_specs, out_specs=out_specs, check_vma=False
    )
```

```python
import jax
import jax.numpy as jnp
from jax import lax
from jax.sharding import Mesh, PartitionSpec as P

D = 5120
FF = 16384
AXES = ("zh", "y", "c", "x", "zl")
SIZES = (4, 4, 2, 4, 4)


def place(*index):
    at = 0
    for i, size in zip(index, SIZES):
        at = at * size + i
    return at


def ring(step):
    return [(i, (i + step) % 4) for i in range(4)]


def swapped(flip):
    return [
        (place(zh, y, c, x, zl), place(x, zl, c ^ flip, zh, y))
        for zh in range(4) for y in range(4) for c in range(2) for x in range(4) for zl in range(4)
    ]


def turned(step):
    return [(y * 4 + zl, (zl + step) % 4 * 4 + y) for y in range(4) for zl in range(4)]


def move(value, axis, step):
    return lax.ppermute(value, axis, ring(step))


def pairs(step):
    return [(i, i ^ step) for i in range(4)]


def joined(value, axis, index):
    for step, later in ((1, index % 2 == 1), (3, index >= 2)):
        got = lax.ppermute(value, axis, pairs(step))
        value = jnp.concatenate([jnp.where(later, got, value), jnp.where(later, value, got)], axis=0)
    return value


def in_three(value):
    terms = []
    for _ in range(3):
        term = lax.reduce_precision(value, 8, 7)
        terms.append(term.astype(jnp.bfloat16))
        value = value - term
    return jnp.stack(terms)


def pack(value, width):
    terms = in_three(value).reshape(-1)
    return jnp.pad(terms, (0, -terms.shape[0] % (8 * width))).reshape(-1, width)


def unpack(rows, size):
    return rows.reshape(-1)[: 3 * size].reshape(3, size).sum(0)


def placed(value, index, count):
    size = value.shape[0]
    return lax.dynamic_update_slice(jnp.zeros((size * count,), value.dtype), value, (index * size,))


def per_device(features, down_weight, member_left, member_right, probe, payoff, opponent):
    f32, bf16 = jnp.float32, jnp.bfloat16
    rows, width = features.shape
    members = member_right.shape[0]
    tokens = rows // members
    population = payoff.shape[0]
    block = down_weight.shape[0]
    cols = probe.shape[0]
    spread = 1.0 / jnp.sqrt(f32(FF))
    zh, y, c, x, zl = (lax.axis_index(a) for a in AXES)
    first = c == 0
    many = 4 * rows

    own = jnp.concatenate([down_weight, member_right], axis=0)
    stack = lax.all_gather(own, ("zh", "c"), axis=0, tiled=True).reshape(4, 2, -1, width)
    weight = stack[:, :, :block].reshape(-1, width)
    rights = lax.all_gather(stack[:, :, block:], "y", axis=0, tiled=False)

    left_cols = lax.dynamic_slice(member_left, (0, (x * 4 + zl) * cols), (members, cols)).astype(f32)
    payload = jnp.concatenate([left_cols, probe[None, :]], axis=0)
    mine = jnp.where(first, payload[:, :block], payload[:, block:])
    other = jnp.where(first, left_cols[:, block:], left_cols[:, :block])
    mine = lax.ppermute(mine, AXES, swapped(0))
    other = lax.ppermute(other, AXES, swapped(1))
    mine, other = lax.optimization_barrier((mine, other))

    direction = jnp.sum(down_weight.astype(f32) * mine[members][:, None], axis=0)
    inner = jnp.sum(
        features.astype(f32).reshape(members, tokens, width) * member_right.astype(f32)[:, None, :],
        axis=2,
    ).reshape(rows)
    left_dot = jnp.sum(left_cols * probe[None, :], axis=1)
    direction = lax.psum(direction, "c")
    early = jnp.concatenate([direction, placed(inner, y, 4), placed(left_dot, y, 4)])
    early = lax.psum(early, "y")

    features, early = lax.optimization_barrier((features, early))
    around = [features] + [move(features, "y", -j) for j in (1, 2, 3)]
    direction, inner, left_dot = jnp.split(early, [width, width + many])
    direction = lax.psum(direction, "zh")

    mine = mine[:members]
    lefts = jnp.where(first, jnp.concatenate([mine, other], 0), jnp.concatenate([other, mine], 0))
    lefts = jnp.pad(lefts.astype(bf16), ((0, 0), (0, 192 - block))).reshape(-1, many)

    along = jnp.stack([
        lax.dot_general(
            in_three(direction), f, (((1,), (1,)), ((), ())), preferred_element_type=f32
        ).sum(0)
        for f in around
    ])
    along = jnp.roll(along, y, axis=0).reshape(many)
    sums = jnp.concatenate([along, inner, left_dot])
    size = sums.shape[0]

    part = lax.dot_general(
        weight, jnp.concatenate(around, axis=0), (((1,), (1,)), ((), ())), preferred_element_type=f32
    ).astype(bf16).reshape(4, cols, many)
    ride = jnp.concatenate([pack(sums, many), lefts], axis=0)
    end = part.shape[1] + ride.shape[0] - lefts.shape[0]
    parts = []
    for k in range(4):
        one = lax.dynamic_index_in_dim(part, lax.rem(x + k, 4), 0, keepdims=False)
        one = jnp.concatenate([one, ride], axis=0)
        parts.append(one if k == 0 else move(one, "x", k))
    total = sum(p[:end].astype(f32) for p in parts)
    lefts = jnp.stack([parts[k][end:] for k in (0, 3, 2, 1)])
    lefts, total = lax.optimization_barrier((lefts, total))
    lefts = joined(jnp.roll(lefts, x, axis=0).reshape(-1, many), "zl", zl)
    ride = pack(unpack(total[cols:], size), cols)

    total = total[:cols].astype(bf16).T.reshape(4, rows, cols)
    parts = []
    for k in range(4):
        one = lax.dynamic_index_in_dim(total, lax.rem(zl + k + 4 - y, 4), 0, keepdims=False)
        one = jnp.concatenate([one, ride], axis=0)
        parts.append(lax.ppermute(one, ("y", "zl"), turned(k)))
    total = sum(p.astype(f32) for p in parts)
    sums = unpack(total[rows:], size)
    total = total[:rows]

    along, inner, left_dot = jnp.split(sums, [many, 2 * many])
    inner = spread * inner
    dots = along + inner * jnp.repeat(left_dot, tokens)
    scale = 0.5 / jnp.sqrt(f32(D))
    score = jnp.mean(jnp.tanh(scale * dots).reshape(4, members, tokens), axis=2)
    score = jnp.stack([jnp.where(first, score, 0.0), jnp.where(first, 0.0, score)], axis=1)
    score = lax.psum(score.reshape(-1), "c")
    score = lax.psum(placed(score, zh, 4), "zh")

    inner = lax.dynamic_slice(inner, (y * rows,), (rows,))
    lowrank = inner.reshape(members, tokens)[:, :, None] * left_cols[:, None, :]
    mixed = (total + lowrank.reshape(rows, cols)).astype(bf16)

    labels = jnp.arange(population, dtype=jnp.int32)
    rival = jnp.sum(jnp.where(opponent[:, None] == labels[None, :], score[None, :], 0.0), axis=1)
    fitness = payoff * (score - rival)
    fitness = fitness.reshape(4, 4, -1).transpose(1, 0, 2).reshape(population, 1)
    scaled = lefts.reshape(population, 192)[:, :block].astype(f32)
    scaled = (fitness * scaled).astype(bf16)
    term = lax.dot_general(
        scaled, rights.reshape(population, width), (((0,), (0,)), ((), ())),
        preferred_element_type=f32,
    )
    return mixed, term / jnp.sqrt(f32(population))


def solution(mesh):
    fine = Mesh(mesh.devices.reshape(SIZES), AXES)
    member, tensor = ("zh", "y", "c"), ("x", "zl")
    in_specs = (
        P(member, tensor), P(member, tensor), P(member, None), P(member, tensor), P(tensor), P(), P(),
    )
    out_specs = (P(member, tensor), P(member, tensor))
    return jax.shard_map(
        per_device, mesh=fine, in_specs=in_specs, out_specs=out_specs, check_vma=False
    )
```

```python
import jax
import jax.numpy as jnp
from jax import lax
from jax.sharding import Mesh, PartitionSpec as P

D = 5120
FF = 16384
AXES = ("zh", "y", "c", "x", "zl")
SIZES = (4, 4, 2, 4, 4)


def place(*index):
    at = 0
    for i, size in zip(index, SIZES):
        at = at * size + i
    return at


def ring(step):
    return [(i, (i + step) % 4) for i in range(4)]


def swapped(flip):
    return [
        (place(zh, y, c, x, zl), place(x, zl, c ^ flip, zh, y))
        for zh in range(4) for y in range(4) for c in range(2) for x in range(4) for zl in range(4)
    ]


def turned():
    return [(y * 4 + zl, zl * 4 + y) for y in range(4) for zl in range(4)]


def move(value, axis, step):
    return lax.ppermute(value, axis, ring(step))


def pairs(step):
    return [(i, i ^ step) for i in range(4)]


def joined(value, axis, index):
    for step, later in ((1, index % 2 == 1), (3, index >= 2)):
        got = lax.ppermute(value, axis, pairs(step))
        value = jnp.concatenate([jnp.where(later, got, value), jnp.where(later, value, got)], axis=0)
    return value


def in_three(value):
    terms = []
    for _ in range(3):
        term = lax.reduce_precision(value, 8, 7)
        terms.append(term.astype(jnp.bfloat16))
        value = value - term
    return jnp.stack(terms)


def pack(value, width):
    terms = in_three(value).reshape(-1)
    return jnp.pad(terms, (0, -terms.shape[0] % (8 * width))).reshape(-1, width)


def unpack(rows, size):
    return rows.reshape(-1)[: 3 * size].reshape(3, size).sum(0)


def placed(value, index, count):
    size = value.shape[0]
    return lax.dynamic_update_slice(jnp.zeros((size * count,), value.dtype), value, (index * size,))


def per_device(features, down_weight, member_left, member_right, probe, payoff, opponent):
    f32, bf16 = jnp.float32, jnp.bfloat16
    rows, width = features.shape
    members = member_right.shape[0]
    tokens = rows // members
    population = payoff.shape[0]
    block = down_weight.shape[0]
    cols = probe.shape[0]
    spread = 1.0 / jnp.sqrt(f32(FF))
    zh, y, c, x, zl = (lax.axis_index(a) for a in AXES)
    first = c == 0
    many = 4 * rows

    weight = lax.all_gather(down_weight, ("zh", "c"), axis=0, tiled=True)
    rights, weight = lax.optimization_barrier((member_right, weight))
    rights = lax.all_gather(rights, ("zh", "y", "c"), axis=0, tiled=True)

    left_cols = lax.dynamic_slice(member_left, (0, (x * 4 + zl) * cols), (members, cols)).astype(f32)
    payload = jnp.concatenate([left_cols, probe[None, :]], axis=0)
    mine = jnp.where(first, payload[:, :block], payload[:, block:])
    other = jnp.where(first, left_cols[:, block:], left_cols[:, :block])
    mine = lax.ppermute(mine, AXES, swapped(0))
    other = lax.ppermute(other, AXES, swapped(1))
    mine, other = lax.optimization_barrier((mine, other))

    direction = jnp.sum(down_weight.astype(f32) * mine[members][:, None], axis=0)
    inner = jnp.sum(
        features.astype(f32).reshape(members, tokens, width) * member_right.astype(f32)[:, None, :],
        axis=2,
    ).reshape(rows)
    left_dot = jnp.sum(left_cols * probe[None, :], axis=1)
    direction = lax.psum(direction, "c")
    early = jnp.concatenate([direction, placed(inner, y, 4), placed(left_dot, y, 4)])
    early = lax.psum(early, "y")

    features, early = lax.optimization_barrier((features, early))
    around = [features] + [move(features, "y", -j) for j in (1, 2, 3)]
    direction, inner, left_dot = jnp.split(early, [width, width + many])
    direction = lax.psum(direction, "zh")

    mine = mine[:members]
    lefts = jnp.where(first, jnp.concatenate([mine, other], 0), jnp.concatenate([other, mine], 0))
    lefts = jnp.pad(lefts.astype(bf16), ((0, 0), (0, 192 - block))).reshape(-1, many)

    along = jnp.stack([
        lax.dot_general(
            in_three(direction), f, (((1,), (1,)), ((), ())), preferred_element_type=f32
        ).sum(0)
        for f in around
    ])
    along = jnp.roll(along, y, axis=0).reshape(many)
    sums = jnp.concatenate([along, inner, left_dot])
    size = sums.shape[0]

    part = lax.dot_general(
        weight, jnp.concatenate(around, axis=0), (((1,), (1,)), ((), ())), preferred_element_type=f32
    ).astype(bf16).reshape(4, cols, many)
    ride = jnp.concatenate([pack(sums, many), lefts], axis=0)
    end = part.shape[1] + ride.shape[0] - lefts.shape[0]
    parts = []
    for k in range(4):
        one = lax.dynamic_index_in_dim(part, lax.rem(x + k, 4), 0, keepdims=False)
        one = jnp.concatenate([one, ride], axis=0)
        parts.append(one if k == 0 else move(one, "x", k))
    total = sum(p[:end].astype(f32) for p in parts)
    lefts = jnp.stack([parts[k][end:] for k in (0, 3, 2, 1)])
    lefts, total = lax.optimization_barrier((lefts, total))
    lefts = joined(jnp.roll(lefts, x, axis=0).reshape(-1, many), "zl", zl)
    ride = pack(unpack(total[cols:], size), cols)

    total = total[:cols].astype(bf16).T.reshape(4, rows, cols)
    parts = []
    for k in range(4):
        one = lax.dynamic_index_in_dim(total, lax.rem(zl + k + 4 - y, 4), 0, keepdims=False)
        one = jnp.concatenate([one, ride], axis=0)
        parts.append(one if k == 0 else move(one, "zl", k))
    total = sum(p.astype(f32) for p in parts)
    sums = unpack(total[rows:], size)
    total = total[:rows].astype(bf16)

    along, inner, left_dot = jnp.split(sums, [many, 2 * many])
    inner = spread * inner
    dots = along + inner * jnp.repeat(left_dot, tokens)
    scale = 0.5 / jnp.sqrt(f32(D))
    score = jnp.mean(jnp.tanh(scale * dots).reshape(4, members, tokens), axis=2)
    score = jnp.stack([jnp.where(first, score, 0.0), jnp.where(first, 0.0, score)], axis=1)
    score = lax.psum(score.reshape(-1), "c")
    score = lax.psum(placed(score, zh, 4), "zh")

    total = lax.ppermute(total, ("y", "zl"), turned()).astype(f32)
    inner = lax.dynamic_slice(inner, (y * rows,), (rows,))
    lowrank = inner.reshape(members, tokens)[:, :, None] * left_cols[:, None, :]
    mixed = (total + lowrank.reshape(rows, cols)).astype(bf16)

    labels = jnp.arange(population, dtype=jnp.int32)
    rival = jnp.sum(jnp.where(opponent[:, None] == labels[None, :], score[None, :], 0.0), axis=1)
    fitness = payoff * (score - rival)
    scaled = lefts.reshape(4, 4, -1, 192)[..., :block].transpose(1, 0, 2, 3)
    scaled = (fitness[:, None] * scaled.reshape(population, block).astype(f32)).astype(bf16)
    term = lax.dot_general(
        scaled, rights, (((0,), (0,)), ((), ())),
        preferred_element_type=f32,
    )
    return mixed, term / jnp.sqrt(f32(population))


def solution(mesh):
    fine = Mesh(mesh.devices.reshape(SIZES), AXES)
    member, tensor = ("zh", "y", "c"), ("x", "zl")
    in_specs = (
        P(member, tensor), P(member, tensor), P(member, None), P(member, tensor), P(tensor), P(), P(),
    )
    out_specs = (P(member, tensor), P(member, tensor))
    return jax.shard_map(
        per_device, mesh=fine, in_specs=in_specs, out_specs=out_specs, check_vma=False
    )
```

```python
import jax
import jax.numpy as jnp
from jax import lax
from jax.sharding import Mesh, PartitionSpec as P

D = 5120
FF = 16384
AXES = ("zh", "y", "c", "x", "zl")
SIZES = (4, 4, 2, 4, 4)


def place(*index):
    at = 0
    for i, size in zip(index, SIZES):
        at = at * size + i
    return at


def ring(step):
    return [(i, (i + step) % 4) for i in range(4)]


def swapped(flip):
    return [
        (place(zh, y, c, x, zl), place(x, zl, c ^ flip, zh, y))
        for zh in range(4) for y in range(4) for c in range(2) for x in range(4) for zl in range(4)
    ]


def turned():
    return [(y * 4 + zl, zl * 4 + y) for y in range(4) for zl in range(4)]


def move(value, axis, step):
    return lax.ppermute(value, axis, ring(step))


def pairs(step):
    return [(i, i ^ step) for i in range(4)]


def joined(value, axis, index):
    for step, later in ((1, index % 2 == 1), (3, index >= 2)):
        got = lax.ppermute(value, axis, pairs(step))
        value = jnp.concatenate([jnp.where(later, got, value), jnp.where(later, value, got)], axis=0)
    return value


def in_three(value):
    terms = []
    for _ in range(3):
        term = lax.reduce_precision(value, 8, 7)
        terms.append(term.astype(jnp.bfloat16))
        value = value - term
    return jnp.stack(terms)


def pack(value, width):
    terms = in_three(value).reshape(-1)
    return jnp.pad(terms, (0, -terms.shape[0] % (8 * width))).reshape(-1, width)


def unpack(rows, size):
    return rows.reshape(-1)[: 3 * size].reshape(3, size).sum(0)


def placed(value, index, count):
    size = value.shape[0]
    return lax.dynamic_update_slice(jnp.zeros((size * count,), value.dtype), value, (index * size,))


def per_device(features, down_weight, member_left, member_right, probe, payoff, opponent):
    f32, bf16 = jnp.float32, jnp.bfloat16
    rows, width = features.shape
    members = member_right.shape[0]
    tokens = rows // members
    population = payoff.shape[0]
    block = down_weight.shape[0]
    cols = probe.shape[0]
    spread = 1.0 / jnp.sqrt(f32(FF))
    zh, y, c, x, zl = (lax.axis_index(a) for a in AXES)
    first = c == 0
    many = 4 * rows

    weight = lax.all_gather(down_weight, ("zh", "c"), axis=0, tiled=True)
    rights, weight = lax.optimization_barrier((member_right, weight))
    rights = lax.all_gather(rights, ("zh", "c"), axis=0, tiled=True).reshape(4, -1, width)
    rights = lax.all_gather(rights, "y", axis=1, tiled=False)

    left_cols = lax.dynamic_slice(member_left, (0, (x * 4 + zl) * cols), (members, cols)).astype(f32)
    payload = jnp.concatenate([left_cols, probe[None, :]], axis=0)
    mine = jnp.where(first, payload[:, :block], payload[:, block:])
    other = jnp.where(first, left_cols[:, block:], left_cols[:, :block])
    mine = lax.ppermute(mine, AXES, swapped(0))
    other = lax.ppermute(other, AXES, swapped(1))
    mine, other = lax.optimization_barrier((mine, other))

    direction = jnp.sum(down_weight.astype(f32) * mine[members][:, None], axis=0)
    inner = jnp.sum(
        features.astype(f32).reshape(members, tokens, width) * member_right.astype(f32)[:, None, :],
        axis=2,
    ).reshape(rows)
    left_dot = jnp.sum(left_cols * probe[None, :], axis=1)
    direction = lax.psum(direction, "c")
    early = jnp.concatenate([direction, placed(inner, y, 4), placed(left_dot, y, 4)])
    early = lax.psum(early, "y")

    features, early = lax.optimization_barrier((features, early))
    around = [features] + [move(features, "y", -j) for j in (1, 2, 3)]
    direction, inner, left_dot = jnp.split(early, [width, width + many])
    direction = lax.psum(direction, "zh")

    mine = mine[:members]
    lefts = jnp.where(first, jnp.concatenate([mine, other], 0), jnp.concatenate([other, mine], 0))
    lefts = jnp.pad(lefts.astype(bf16), ((0, 0), (0, 192 - block))).reshape(-1, many)

    along = jnp.stack([
        lax.dot_general(
            in_three(direction), f, (((1,), (1,)), ((), ())), preferred_element_type=f32
        ).sum(0)
        for f in around
    ])
    along = jnp.roll(along, y, axis=0).reshape(many)
    sums = jnp.concatenate([along, inner, left_dot])
    size = sums.shape[0]

    part = lax.dot_general(
        weight, jnp.concatenate(around, axis=0), (((1,), (1,)), ((), ())), preferred_element_type=f32
    ).astype(bf16).reshape(4, cols, many)
    ride = jnp.concatenate([pack(sums, many), lefts], axis=0)
    end = part.shape[1] + ride.shape[0] - lefts.shape[0]
    parts = []
    for k in range(4):
        one = lax.dynamic_index_in_dim(part, lax.rem(x + k, 4), 0, keepdims=False)
        one = jnp.concatenate([one, ride], axis=0)
        parts.append(one if k == 0 else move(one, "x", k))
    total = sum(p[:end].astype(f32) for p in parts)
    lefts = jnp.stack([parts[k][end:] for k in (0, 3, 2, 1)])
    lefts, total = lax.optimization_barrier((lefts, total))
    lefts = joined(jnp.roll(lefts, x, axis=0).reshape(-1, many), "zl", zl)
    ride = pack(unpack(total[cols:], size), cols)

    total = total[:cols].astype(bf16).T.reshape(4, rows, cols)
    parts = []
    for k in range(4):
        one = lax.dynamic_index_in_dim(total, lax.rem(zl + k + 4 - y, 4), 0, keepdims=False)
        one = jnp.concatenate([one, ride], axis=0)
        parts.append(one if k == 0 else move(one, "zl", k))
    total = sum(p.astype(f32) for p in parts)
    sums = unpack(total[rows:], size)
    total = total[:rows].astype(bf16)

    along, inner, left_dot = jnp.split(sums, [many, 2 * many])
    inner = spread * inner
    dots = along + inner * jnp.repeat(left_dot, tokens)
    scale = 0.5 / jnp.sqrt(f32(D))
    score = jnp.mean(jnp.tanh(scale * dots).reshape(4, members, tokens), axis=2)
    score = jnp.stack([jnp.where(first, score, 0.0), jnp.where(first, 0.0, score)], axis=1)
    score = lax.psum(score.reshape(-1), "c")
    score = lax.psum(placed(score, zh, 4), "zh")

    total = lax.ppermute(total, ("y", "zl"), turned()).astype(f32)
    inner = lax.dynamic_slice(inner, (y * rows,), (rows,))
    lowrank = inner.reshape(members, tokens)[:, :, None] * left_cols[:, None, :]
    mixed = (total + lowrank.reshape(rows, cols)).astype(bf16)

    labels = jnp.arange(population, dtype=jnp.int32)
    rival = jnp.sum(jnp.where(opponent[:, None] == labels[None, :], score[None, :], 0.0), axis=1)
    fitness = payoff * (score - rival)
    scaled = lefts.reshape(4, 4, -1, 192)[..., :block].transpose(1, 0, 2, 3)
    scaled = (fitness[:, None] * scaled.reshape(population, block).astype(f32)).astype(bf16)
    term = lax.dot_general(
        scaled, rights.reshape(population, width), (((0,), (0,)), ((), ())),
        preferred_element_type=f32,
    )
    return mixed, term / jnp.sqrt(f32(population))


def solution(mesh):
    fine = Mesh(mesh.devices.reshape(SIZES), AXES)
    member, tensor = ("zh", "y", "c"), ("x", "zl")
    in_specs = (
        P(member, tensor), P(member, tensor), P(member, None), P(member, tensor), P(tensor), P(), P(),
    )
    out_specs = (P(member, tensor), P(member, tensor))
    return jax.shard_map(
        per_device, mesh=fine, in_specs=in_specs, out_specs=out_specs, check_vma=False
    )
```
